128 devices in a mesh: ep: 4 (over y), tp: 32 (over z, x, core).
Axes of the slice: x: 4, y: 4, z: 4, core: 2. Of those that a mesh axis runs over, the one named last changes fastest.
Arguments:
- tokens: bfloat16 [1024, 6144], P('ep', 'tp'), may hold values from -6 to 6
- expert_ids: int32 [1024, 2], P('ep'), may hold values from 0 to 3, as said below
- slot_ids: int32 [1024, 2], P('ep'), may hold values from 0 to 159, as said below
- route_logits: float32 [1024, 2], P('ep'), may hold values from -6 to 6
- gate_weight: bfloat16 [4, 6144, 8192], P('ep', None, 'tp'), may hold values from -0.15625 to 0.15625
- up_weight: bfloat16 [4, 6144, 8192], P('ep', None, 'tp'), may hold values from -0.078125 to 0.078125
- down_weight: bfloat16 [4, 8192, 6144], P('ep', 'tp'), may hold values from -0.125 to 0.125
- out_grad: bfloat16 [1024, 6144], P('ep', 'tp'), may hold values from -8 to 8
Outputs:
- mixed: bfloat16 [1024, 6144], P('ep', 'tp')
- token_grad: bfloat16 [1024, 6144], P('ep', 'tp')
- logit_grad: float32 [1024, 2], P('ep')
- gate_grad: bfloat16 [4, 6144, 8192], P('ep', None, 'tp')
- up_grad: bfloat16 [4, 6144, 8192], P('ep', None, 'tp')
- down_grad: bfloat16 [4, 8192, 6144], P('ep', 'tp')
The draws below stay inside these ranges and needn't reach their ends.
Inputs may be any that keep to these rules, and one draw needn't show every extreme that they name: `expert_ids`: each token names two different experts. In each group of 256 consecutive tokens no expert is named by more than 160 tokens, and one expert, the same in every group, is named by exactly 160. `slot_ids`: within a group of 256 consecutive tokens, the choices of one expert hold the rows 0, 1, ... up to their number less one, given in order over the group's first choices in token order and then over its second choices.
All inputs are finite; a program needn't handle non-finite values.
Results may differ from the reference program's by a relative error of at most 0.025.
Values may be sent and summed in bfloat16 or wider, within the bound.
No kernel may reach another device: no remote copies, remote signals or barrier semaphores. Data moves between devices by JAX's collectives and lax.ppermute only.
A program may use at most 192 MiB of HBM per device.

```python
import jax
import jax.numpy as jnp
from jax import lax

D = 6144
FF = 8192
TOK_GRP = 256
EXPERTS = 4
C_SRC = 160
TOKENS = 1024
N_EP = 4
N_TP = 32


def route_table(key):
    groups = TOKENS // TOK_GRP
    spread = EXPERTS - 1
    hot_expert = jax.random.randint(jax.random.fold_in(key, 11), (), 0, EXPERTS)

    def one_group(group_index):
        group_key = jax.random.fold_in(key, 1000 + group_index)
        ordering = jax.random.permutation(jax.random.fold_in(group_key, 1), TOK_GRP)
        position = jnp.arange(TOK_GRP, dtype=jnp.int32)
        first_pick = jax.random.randint(jax.random.fold_in(group_key, 2), (TOK_GRP,), 0, spread)
        step_pick = jax.random.randint(jax.random.fold_in(group_key, 3), (TOK_GRP,), 0, spread - 1)
        is_hot = position < C_SRC
        hot_other = (hot_expert + 1 + position % spread) % EXPERTS
        cold_first = (hot_expert + 1 + first_pick) % EXPERTS
        cold_second = (hot_expert + 1 + (first_pick + 1 + step_pick) % spread) % EXPERTS
        choice_one = jnp.where(is_hot, hot_expert, cold_first)
        choice_two = jnp.where(is_hot, hot_other, cold_second)
        flip_bit = jax.random.randint(jax.random.fold_in(group_key, 4), (TOK_GRP,), 0, 2)
        chosen = jnp.where(flip_bit[:, None] == 1, jnp.stack([choice_two, choice_one], axis=1), jnp.stack([choice_one, choice_two], axis=1))
        return jnp.zeros((TOK_GRP, 2), jnp.int32).at[ordering].set(chosen.astype(jnp.int32))
    chosen_ids = jax.vmap(one_group)(jnp.arange(groups, dtype=jnp.int32))
    flat_ids = jnp.transpose(chosen_ids, (0, 2, 1)).reshape(groups, 2 * TOK_GRP)
    onehot = (flat_ids[:, :, None] == jnp.arange(EXPERTS, dtype=jnp.int32)[None, None, :]).astype(jnp.int32)
    running = jnp.cumsum(onehot, axis=1) - onehot
    slot_flat = jnp.sum(running * onehot, axis=2)
    slot_table = jnp.transpose(slot_flat.reshape(groups, 2, TOK_GRP), (0, 2, 1)).reshape(TOKENS, 2)
    return (chosen_ids.reshape(TOKENS, 2), slot_table.astype(jnp.int32))


def draw_expert_ids(key, part):
    chosen_ids, slot_table = route_table(key)
    return chosen_ids


def draw_slot_ids(key, part):
    chosen_ids, slot_table = route_table(key)
    return slot_table


def draw_out_grad(key, part):
    key = jax.random.fold_in(key, 7)
    columns = jnp.arange(D, dtype=jnp.float32) / D
    base = jnp.clip(jax.random.normal(key, (TOKENS, D), jnp.float32), -4.0, 4.0)
    factor = jnp.exp(jnp.log(3.0) * columns) / 1.7
    return (base * factor[None, :]).astype(jnp.bfloat16)


def raised(array, key, source, target, shards_of, factor):
    owner, partner = [(jnp.arange(array.shape[dim]) // (array.shape[dim] // shards_of)).reshape([-1 if axis == dim else 1 for axis in range(array.ndim)]) for dim in (source, target)]
    chosen = jax.random.permutation(key, shards_of)[partner]
    strong = (owner == chosen) | (owner == (partner + shards_of // 2) % shards_of)
    return jnp.where(strong, factor * array, array)


def block_scale(key, shape, pieces, smallest, high):
    def one(dim, blocks):
        draws = jax.random.uniform(jax.random.fold_in(jax.random.fold_in(key, 6), dim), (blocks,), jnp.float32, smallest / len(pieces), high / len(pieces))
        return jnp.repeat(jnp.exp(draws), shape[dim] // blocks).reshape((-1,) + (1,) * (len(shape) - dim - 1))

    loudness = one(*pieces[0])
    for cut in pieces[1:]:
        loudness = loudness * one(*cut)
    return loudness


def centred(own_key, shape, scale, most, cuts=(), held_as=jnp.bfloat16):
    entries = jax.random.normal(own_key, shape, jnp.float32) * scale
    if len(cuts) > 0:
        entries = block_scale(own_key, shape, cuts, -0.22, 0.18) * entries
    return jnp.clip(entries, min=-most, max=most).astype(held_as)


def gaussian_with(rng, shape, scale, most, split, heavy, kind=jnp.bfloat16):
    entries = scale * jax.random.normal(rng, shape, jnp.float32)
    if split:
        entries = entries * block_scale(rng, shape, split, -0.22, 0.18)
    return jnp.clip(raised(entries, jax.random.fold_in(rng, 3), *heavy), -most, most).astype(kind)


def setup_inputs(seed: int = 0) -> dict:
    splits = jax.random.split(jax.random.key(seed), 9)
    return {
        "tokens": centred(splits[0], (TOKENS, D), 1.0, 6.0, ((0, 4), (1, 32))),
        "expert_ids": draw_expert_ids(jax.random.fold_in(splits[8], 71), 0),
        "slot_ids": draw_slot_ids(jax.random.fold_in(splits[8], 71), 0),
        "route_logits": centred(splits[3], (TOKENS, 2), 2.0, 6.0, ((0, 4),), jnp.float32),
        "gate_weight": gaussian_with(splits[4], (EXPERTS, D, FF), D ** -0.5, 0.15625, ((0, 4), (2, 32)), (2, 1, 32, 2.75)),
        "up_weight": centred(splits[5], (EXPERTS, D, FF), D ** -0.5, 0.078125, ((0, 4), (2, 32))),
        "down_weight": gaussian_with(splits[6], (EXPERTS, FF, D), FF ** -0.5, 0.125, ((0, 4), (1, 32)), (1, 2, 32, 2.75)),
        "out_grad": draw_out_grad(jax.random.fold_in(splits[8], 71), 0),
    }


def blocked_out(hidden, down_rows):
    width = FF // N_TP

    def add_block(total, block_index):
        begin = (block_index * width).astype(jnp.int32)
        part_rows = lax.dynamic_slice_in_dim(hidden, begin, width, 1)
        part_down = lax.dynamic_slice_in_dim(down_rows, begin, width, 0)
        term = jnp.dot(part_rows, part_down, preferred_element_type=jnp.float32)
        rounded = lax.optimization_barrier(term.astype(jnp.bfloat16))
        return total + rounded.astype(jnp.float32), None

    start = jnp.zeros((hidden.shape[0], down_rows.shape[1]), jnp.float32)
    total, _ = lax.scan(add_block, start, jnp.arange(N_TP, dtype=jnp.int32))
    return total.astype(jnp.bfloat16)


def blocked_back(gate_rows, up_rows, gate_mat, up_mat):
    width = FF // N_TP
    dims = (((1,), (1,)), ((), ()))

    def add_block(total, block_index):
        begin = (block_index * width).astype(jnp.int32)
        part_gate = lax.dynamic_slice_in_dim(gate_rows, begin, width, 1)
        part_up = lax.dynamic_slice_in_dim(up_rows, begin, width, 1)
        mat_gate = lax.dynamic_slice_in_dim(gate_mat, begin, width, 1)
        mat_up = lax.dynamic_slice_in_dim(up_mat, begin, width, 1)
        term = lax.dot_general(part_gate, mat_gate, dims, preferred_element_type=jnp.float32)
        term = term + lax.dot_general(part_up, mat_up, dims, preferred_element_type=jnp.float32)
        rounded = lax.optimization_barrier(term.astype(jnp.bfloat16))
        return total + rounded.astype(jnp.float32), None

    start = jnp.zeros((gate_rows.shape[0], gate_mat.shape[0]), jnp.float32)
    total, _ = lax.scan(add_block, start, jnp.arange(N_TP, dtype=jnp.int32))
    return total.astype(jnp.bfloat16)


def reference(tokens, expert_ids, slot_ids, route_logits, gate_weight, up_weight, down_weight, out_grad):
    rows_all = N_EP * C_SRC
    token_index = jnp.arange(TOKENS, dtype=jnp.int32)
    group_of = token_index // TOK_GRP
    target = (expert_ids * rows_all + group_of[:, None] * C_SRC + slot_ids).astype(jnp.int32)
    shares = jnp.stack([jax.nn.sigmoid(route_logits[:, 0] - route_logits[:, 1]),
                        jax.nn.sigmoid(route_logits[:, 1] - route_logits[:, 0])], axis=1)
    source = jnp.zeros((EXPERTS * rows_all,), jnp.int32).at[target.reshape(-1)].set(jnp.repeat(token_index + 1, 2))
    weight_flat = jnp.zeros((EXPERTS * rows_all,), jnp.float32).at[target.reshape(-1)].set(shares.reshape(-1))
    padded_in = jnp.concatenate([jnp.zeros((1, D), jnp.bfloat16), tokens], 0)
    padded_grad = jnp.concatenate([jnp.zeros((1, D), jnp.bfloat16), out_grad], 0)
    expert_in = padded_in[source].reshape(EXPERTS, rows_all, D)
    expert_grad_in = (weight_flat[:, None] * padded_grad[source].astype(jnp.float32)).astype(jnp.bfloat16)
    expert_grad_in = expert_grad_in.reshape(EXPERTS, rows_all, D)
    rows_dims = (((0,), (0,)), ((), ()))
    outputs, backs, gate_list, up_list, down_list = [], [], [], [], []
    for expert in range(EXPERTS):
        rows_in = expert_in[expert]
        rows_grad = expert_grad_in[expert]
        gate_act = jnp.dot(rows_in, gate_weight[expert], preferred_element_type=jnp.float32)
        up_act = jnp.dot(rows_in, up_weight[expert], preferred_element_type=jnp.float32)
        sigmoid_gate = jax.nn.sigmoid(gate_act)
        hidden = (gate_act * sigmoid_gate * up_act).astype(jnp.bfloat16)
        outputs.append(blocked_out(hidden, down_weight[expert]))
        hidden_grad = lax.dot_general(rows_grad, down_weight[expert], (((1,), (1,)), ((), ())),
                                      preferred_element_type=jnp.float32)
        up_rows = (hidden_grad * gate_act * sigmoid_gate).astype(jnp.bfloat16)
        gate_rows = (hidden_grad * up_act * sigmoid_gate * (1.0 + gate_act * (1.0 - sigmoid_gate))).astype(jnp.bfloat16)
        down_list.append(lax.dot_general(hidden, rows_grad, rows_dims, preferred_element_type=jnp.float32).astype(jnp.bfloat16))
        gate_list.append(lax.dot_general(rows_in, gate_rows, rows_dims, preferred_element_type=jnp.float32).astype(jnp.bfloat16))
        up_list.append(lax.dot_general(rows_in, up_rows, rows_dims, preferred_element_type=jnp.float32).astype(jnp.bfloat16))
        backs.append(blocked_back(gate_rows, up_rows, gate_weight[expert], up_weight[expert]))
    expert_out = jnp.stack(outputs).reshape(EXPERTS * rows_all, D)
    expert_back = jnp.stack(backs).reshape(EXPERTS * rows_all, D)
    picked = expert_out[target].astype(jnp.float32)
    mixed = jnp.sum(shares[:, :, None] * picked, axis=1).astype(jnp.bfloat16)
    route_product = jnp.sum(out_grad.astype(jnp.float32)[:, None, :] * picked, axis=2)
    cross = shares[:, 0] * shares[:, 1] * (route_product[:, 0] - route_product[:, 1])
    logit_grad = jnp.stack([cross, -cross], axis=1)
    token_grad = jnp.sum(expert_back[target].astype(jnp.float32), axis=1).astype(jnp.bfloat16)
    return (mixed, token_grad, logit_grad, jnp.stack(gate_list), jnp.stack(up_list), jnp.stack(down_list))
```

```python
import jax
import jax.numpy as jnp
from jax import lax
from jax.experimental import pallas as pl
from jax.experimental.pallas import tpu as pltpu
from jax.sharding import Mesh, PartitionSpec as P

CAP = 160
SIDE = 4
WIDE = 192
HID = 256
ROWS = SIDE * CAP
BLOCKS = 32
EXTRA = 16
TP = ("z", "x", "c")
BF = jnp.bfloat16
F32 = jnp.float32
VMEM_LIMIT = 48 * 1024 * 1024


def ring(shift):
    return [(i, (i + shift) % SIDE) for i in range(SIDE)]


def plane(phase, shift):
    pairs = []
    for z in range(SIDE):
        for x in range(SIDE):
            for c in range(2):
                along_z = (phase == 1) == (c == 0)
                to_z, to_x = ((z + shift) % SIDE, x) if along_z else (z, (x + shift) % SIDE)
                pairs.append(((z * SIDE + x) * 2 + c, (to_z * SIDE + to_x) * 2 + c))
    return pairs


def send(value, phase, shift):
    return lax.ppermute(value, TP, plane(phase, shift))


def swap(value):
    return lax.ppermute(value, "c", [(0, 1), (1, 0)])


def dot(a, b, dims=((1,), (0,))):
    return lax.dot_general(a, b, (dims, ((), ())), preferred_element_type=F32)


def whole(kernel, ins, outs, flops, name):
    specs, arrays = [], []
    for array, block, at in ins:
        shape = block or array.shape
        rest = (0,) * (len(shape) - 1)
        specs.append(pl.BlockSpec(shape, lambda i, at=at, rest=rest: (at, *rest)))
        arrays.append(array)
    moved = sum(s.size * s.dtype.itemsize for s in outs)
    for array, block, _ in ins:
        size = array.size if block is None else block[0] * block[1] * block[2]
        moved += size * array.dtype.itemsize
    return pl.pallas_call(
        kernel,
        grid=(1,),
        in_specs=specs,
        out_specs=[
            pl.BlockSpec(s.shape, lambda i, n=len(s.shape): (0,) * n) for s in outs
        ],
        out_shape=outs,
        compiler_params=pltpu.CompilerParams(vmem_limit_bytes=VMEM_LIMIT),
        cost_estimate=pl.CostEstimate(flops=flops, bytes_accessed=moved, transcendentals=0),
        name=name,
    )(*arrays)


def shape_of(*dims, dtype=BF):
    return jax.ShapeDtypeStruct(dims, dtype)


def pack(flat_t, logits_t, tokens, out_grad):
    def kernel(flat, logits, tok, grad, *outs):
        gap = logits[0:1, :] - logits[1:2, :]
        share0, share1 = jax.nn.sigmoid(gap), jax.nn.sigmoid(-gap)
        for j in range(SIDE):
            slot = lax.broadcasted_iota(jnp.int32, (CAP, flat.shape[1]), 0) + CAP * j
            first, second = slot == flat[0:1, :], slot == flat[1:2, :]
            pick = jnp.where(first | second, 1.0, 0.0).astype(BF)
            weight = jnp.sum(
                jnp.where(first, share0, 0.0) + jnp.where(second, share1, 0.0),
                axis=1,
                keepdims=True,
            )
            outs[j][:, :WIDE] = dot(pick, tok[...]).astype(BF)
            outs[j][:, WIDE:] = (weight * dot(pick, grad[...])).astype(BF)

    return whole(
        kernel,
        [(a, None, 0) for a in (flat_t, logits_t, tokens, out_grad)],
        [shape_of(CAP, 2 * WIDE)] * SIDE,
        4 * ROWS * 256 * WIDE,
        "pack_rows",
    )


def assemble(parts):
    def kernel(*refs):
        rows = jnp.concatenate([r[...] for r in refs[:SIDE]], axis=0)
        cols = rows.T
        refs[SIDE][...] = cols[:WIDE]
        refs[SIDE + 1][...] = cols[WIDE:]

    return whole(
        kernel,
        [(p, None, 0) for p in parts],
        [shape_of(WIDE, ROWS)] * 2,
        0,
        "assemble_columns",
    )


def arrange(order, gate, up, down):
    def kernel(order_ref, gate_in, up_in, down_in, gate_out, up_out, down_out):
        gate_out[...] = gate_in[...]
        up_out[...] = up_in[...]
        turned = down_in[...].T
        odd = lax.rem(order_ref[pl.program_id(0)], 2) == 1
        down_out[0] = jnp.where(odd, turned[WIDE:], turned[:WIDE])

    picked = pl.BlockSpec((1, WIDE, HID), lambda i, order_ref: (order_ref[i], 0, 0))
    placed = pl.BlockSpec((1, WIDE, HID), lambda i, order_ref: (i, 0, 0))
    return pl.pallas_call(
        kernel,
        grid_spec=pltpu.PrefetchScalarGridSpec(
            num_scalar_prefetch=1,
            grid=(BLOCKS,),
            in_specs=[
                picked,
                picked,
                pl.BlockSpec((HID, 2 * WIDE), lambda i, order_ref: (0, order_ref[i] // 2)),
            ],
            out_specs=[placed] * 3,
        ),
        out_shape=[shape_of(BLOCKS, WIDE, HID)] * 3,
        compiler_params=pltpu.CompilerParams(vmem_limit_bytes=VMEM_LIMIT),
        cost_estimate=pl.CostEstimate(
            flops=0, bytes_accessed=7 * BLOCKS * WIDE * HID * 2, transcendentals=0
        ),
        name="arrange_weights",
    )(order, gate, up, down)


def contract(weights, own, other, totals, index):
    count = len(own)
    blocks = SIDE // count

    def kernel(*refs):
        refs = list(refs)
        pieces = [refs.pop(0)[...].reshape(blocks * WIDE, ROWS) for _ in range(2 * count)]
        mats = [[refs.pop(0)[...], refs.pop(0)[...]] for _ in weights]
        before = [refs.pop(0) for _ in totals]
        for w, (out, (mat_own, mat_other)) in enumerate(zip(refs, mats)):
            parts = [
                m[k * blocks : (k + 1) * blocks].reshape(blocks * WIDE, HID)
                for m in (mat_own, mat_other)
                for k in range(count)
            ]
            total = before[w][...] if totals else 0.0
            for mat, piece in zip(parts, pieces):
                total += dot(mat, piece, ((0,), (0,)))
            out[...] = total

    block = (SIDE, WIDE, HID)
    ins = [(a, None, 0) for a in (*own, *other)]
    for w in weights:
        ins += [(w, block, index), (w, block, SIDE + index)]
    ins += [(t, None, 0) for t in totals]
    return whole(
        kernel,
        ins,
        [shape_of(HID, ROWS, dtype=F32)] * len(weights),
        len(weights) * 2 * 2 * SIDE * WIDE * HID * ROWS,
        "contract_features",
    )


def activate(gate_act, up_act):
    def kernel(gate, up, out):
        g = gate[...]
        out[...] = (g * jax.nn.sigmoid(g) * up[...]).astype(BF)

    return whole(
        kernel, [(gate_act, None, 0), (up_act, None, 0)], [shape_of(HID, ROWS)], 0, "hidden"
    )[0]


def differentiate(hidden, gate_act, up_act, hidden_grad):
    def kernel(hid, gate, up, grad, out):
        g, hg = gate[...], grad[...]
        s = jax.nn.sigmoid(g)
        out[0:HID] = (hg * up[...] * s * (1.0 + g * (1.0 - s))).astype(BF)
        out[HID : 2 * HID] = (hg * g * s).astype(BF)
        product = hid[...].astype(F32) * hg
        out[2 * HID :] = jnp.sum(
            product.reshape(HID // EXTRA, EXTRA, ROWS), axis=0
        ).astype(BF)

    return whole(
        kernel,
        [(a, None, 0) for a in (hidden, gate_act, up_act, hidden_grad)],
        [shape_of(2 * HID + EXTRA, ROWS)],
        0,
        "rows_of_gradient",
    )[0]


def expand(weights, acts, adds, index, split, extra, name):
    pairs = len(weights)
    height = WIDE + (EXTRA if extra else 0)

    def kernel(*refs):
        refs = list(refs)
        mats = [(refs.pop(0), refs.pop(0)) for _ in range(pairs)]
        act = [refs.pop(0), refs.pop(0)]
        arrived = [(refs.pop(0), first) for _, first in adds]
        if extra:
            tail = act[0][pairs * HID :].astype(F32) + act[1][pairs * HID :].astype(F32)
        for b in range(SIDE):
            value = 0.0
            for w, pair in enumerate(mats):
                for mat, a in zip(pair, act):
                    value += dot(mat[b], a[w * HID : (w + 1) * HID])
            ends = tail if extra else None
            for ref, first in arrived:
                if first <= b < first + ref.shape[0]:
                    value += ref[b - first, :WIDE].astype(F32)
                    if extra:
                        ends = ends + ref[b - first, WIDE:].astype(F32)
            out, at = refs[b // split], b % split
            if split == 1:
                out[:WIDE] = value.astype(BF)
                if extra:
                    out[WIDE:] = ends.astype(BF)
            else:
                out[at, :WIDE] = value.astype(BF)
                if extra:
                    out[at, WIDE:] = ends.astype(BF)

    block = (SIDE, WIDE, HID)
    ins = []
    for own, other in weights:
        ins += [(own, block, index), (other, block, index)]
    ins += [(a, None, 0) for a in acts]
    ins += [(a, None, 0) for a, _ in adds]
    dims = (height, ROWS) if split == 1 else (split, height, ROWS)
    return whole(
        kernel,
        ins,
        [shape_of(*dims)] * (SIDE // split),
        pairs * 2 * 2 * SIDE * WIDE * HID * ROWS,
        name,
    )


def gather_sum(parts):
    height = parts[0].shape[0]

    def kernel(*refs):
        total = sum(r[...].astype(F32) for r in refs[:SIDE])
        rows = total.T.astype(BF)
        for j in range(SIDE):
            refs[SIDE + j][...] = rows[j * CAP : (j + 1) * CAP]

    return whole(
        kernel, [(p, None, 0) for p in parts], [shape_of(CAP, height)] * SIDE, 0, "sum_rows"
    )


def mix(flat, logits, parts):
    def kernel(flat_ref, logit_ref, *refs):
        gap = logit_ref[:, 0:1] - logit_ref[:, 1:2]
        share0, share1 = jax.nn.sigmoid(gap), jax.nn.sigmoid(-gap)
        total = 0.0
        for j in range(SIDE):
            slot = lax.broadcasted_iota(jnp.int32, (flat_ref.shape[0], CAP), 1) + CAP * j
            weight = jnp.where(slot == flat_ref[:, 0:1], share0, 0.0) + jnp.where(
                slot == flat_ref[:, 1:2], share1, 0.0
            )
            high = weight.astype(BF)
            low = (weight - high.astype(F32)).astype(BF)
            rows = refs[j][...]
            total += dot(high, rows) + dot(low, rows)
        refs[SIDE][...] = total.astype(BF)

    tokens = flat.shape[0]
    return whole(
        kernel,
        [(a, None, 0) for a in (flat, logits, *parts)],
        [shape_of(tokens, WIDE)],
        4 * tokens * ROWS * WIDE,
        "mix_rows",
    )[0]


def collect(flat, logits, parts):
    def kernel(flat_ref, logit_ref, *refs):
        gap = logit_ref[:, 0:1] - logit_ref[:, 1:2]
        share0, share1 = jax.nn.sigmoid(gap), jax.nn.sigmoid(-gap)
        first, second = 0.0, 0.0
        for j in range(SIDE):
            slot = lax.broadcasted_iota(jnp.int32, (flat_ref.shape[0], CAP), 1) + CAP * j
            rows = refs[j][...]
            first += dot(jnp.where(slot == flat_ref[:, 0:1], 1.0, 0.0).astype(BF), rows)
            second += dot(jnp.where(slot == flat_ref[:, 1:2], 1.0, 0.0).astype(BF), rows)
        refs[SIDE][...] = (first[:, :WIDE] + second[:, :WIDE]).astype(BF)
        product0 = jnp.sum(first[:, WIDE:], axis=1, keepdims=True)
        product1 = jnp.sum(second[:, WIDE:], axis=1, keepdims=True)
        cross = share1 * product0 - share0 * product1
        refs[SIDE + 1][...] = jnp.concatenate([cross, -cross], axis=1)

    tokens = flat.shape[0]
    return whole(
        kernel,
        [(a, None, 0) for a in (flat, logits, *parts)],
        [shape_of(tokens, WIDE), shape_of(tokens, 2, dtype=F32)],
        4 * tokens * ROWS * (WIDE + EXTRA),
        "collect_rows",
    )


PIECES = ((0, 4), (4, 4), (12, 4), (8, 2), (10, 2))


def weight_grads(order, own, other, rows):
    pieces = [(p, base) for base, side in ((0, own), (16, other)) for p in side]
    starts = [(base + first, n) for base in (0, 16) for first, n in PIECES]

    def kernel(order_ref, rows_ref, *refs):
        count = len(pieces)
        ins, outs = refs[:count], refs[count : count + 2]
        held, done, in_sem, out_sem = refs[count + 2 :]
        held_in = held.at[0]
        loads = []
        for k, (first, n) in enumerate(starts):
            loads.append(
                pltpu.make_async_copy(ins[k], held_in.at[pl.ds(first, n)], in_sem.at[k])
            )
            loads[-1].start()
        stores = []
        for k, (first, n) in enumerate(starts):
            loads[k].wait()
            piece = held[0, first : first + n].reshape(n * WIDE, ROWS)
            for w in range(2):
                act = rows_ref[w * HID : (w + 1) * HID]
                done[w, first : first + n] = (
                    dot(piece, act, ((1,), (1,))).astype(BF).reshape(n, WIDE, HID)
                )
                for b in range(first, first + n):
                    stores.append(
                        pltpu.make_async_copy(
                            done.at[w, b], outs[w].at[order_ref[b]], out_sem.at[w, b]
                        )
                    )
                    stores[-1].start()
        for copy in stores:
            copy.wait()

    return pl.pallas_call(
        kernel,
        in_specs=[
            pl.BlockSpec(memory_space=pltpu.SMEM),
            pl.BlockSpec(memory_space=pltpu.VMEM),
        ]
        + [pl.BlockSpec(memory_space=pl.ANY)] * len(pieces),
        out_specs=[pl.BlockSpec(memory_space=pl.ANY)] * 2,
        out_shape=[shape_of(BLOCKS, WIDE, HID)] * 2,
        scratch_shapes=[
            pltpu.VMEM((1, BLOCKS, WIDE, ROWS), BF),
            pltpu.VMEM((2, BLOCKS, WIDE, HID), BF),
            pltpu.SemaphoreType.DMA((len(pieces),)),
            pltpu.SemaphoreType.DMA((2, BLOCKS)),
        ],
        compiler_params=pltpu.CompilerParams(vmem_limit_bytes=VMEM_LIMIT),
        cost_estimate=pl.CostEstimate(
            flops=4 * BLOCKS * WIDE * HID * ROWS,
            bytes_accessed=2 * BLOCKS * WIDE * (ROWS + 2 * HID),
            transcendentals=0,
        ),
        name="weight_gradients",
    )(order, rows, *[p for p, _ in pieces])


def down_grads(order, own, other, hidden):
    pieces = [*own, *other]
    starts = [(base + first, n) for base in (0, 16) for first, n in PIECES]

    def kernel(order_ref, hidden_ref, *refs):
        count = len(pieces)
        ins, out = refs[:count], refs[count]
        held, placed, done, in_sem, out_sem = refs[count + 1 :]
        loads = []
        for k, (first, n) in enumerate(starts):
            loads.append(
                pltpu.make_async_copy(ins[k], held.at[pl.ds(first, n)], in_sem.at[k])
            )
            loads[-1].start()
        for k, (first, n) in enumerate(starts):
            loads[k].wait()
            for b in range(first, first + n):
                placed[order_ref[b]] = dot(hidden_ref[...], held[b], ((1,), (1,))).astype(BF)
        stores = []
        for s in range(BLOCKS // 2):
            done[s] = jnp.concatenate([placed[2 * s], placed[2 * s + 1]], axis=1)
            stores.append(
                pltpu.make_async_copy(
                    done.at[s], out.at[:, pl.ds(s * 2 * WIDE, 2 * WIDE)], out_sem.at[s]
                )
            )
            stores[-1].start()
        for copy in stores:
            copy.wait()

    return pl.pallas_call(
        kernel,
        in_specs=[
            pl.BlockSpec(memory_space=pltpu.SMEM),
            pl.BlockSpec(memory_space=pltpu.VMEM),
        ]
        + [pl.BlockSpec(memory_space=pl.ANY)] * len(pieces),
        out_specs=pl.BlockSpec(memory_space=pl.ANY),
        out_shape=shape_of(HID, BLOCKS * WIDE),
        scratch_shapes=[
            pltpu.VMEM((BLOCKS, WIDE, ROWS), BF),
            pltpu.VMEM((BLOCKS, HID, WIDE), BF),
            pltpu.VMEM((BLOCKS // 2, HID, 2 * WIDE), BF),
            pltpu.SemaphoreType.DMA((len(pieces),)),
            pltpu.SemaphoreType.DMA((BLOCKS // 2,)),
        ],
        compiler_params=pltpu.CompilerParams(vmem_limit_bytes=VMEM_LIMIT),
        cost_estimate=pl.CostEstimate(
            flops=2 * BLOCKS * WIDE * HID * ROWS,
            bytes_accessed=2 * BLOCKS * WIDE * (ROWS + HID),
            transcendentals=0,
        ),
        name="down_gradients",
    )(order, hidden, *pieces)


def spread(block):
    arrived = [send(block, 1, k) for k in (1, 2, 3)]
    near = jnp.stack([block, *arrived])
    after, before = send(near, 2, 1), send(near, 2, 3)
    far_a = send(after[0:2], 2, 1)
    far_b = send(before[2:4], 2, 3)
    return [near, after, before, far_a, far_b]


def reduce(weights, acts, extra, name):
    def part(index, adds, split):
        return expand(weights, acts, adds, index, split, extra, name)

    far_a, far_b = part(2, [], 2)
    from_after = send(far_a, 2, 3)
    from_before = send(far_b, 2, 1)
    (to_before,) = part(1, [(from_after, 0)], 4)
    (to_after,) = part(3, [(from_before, 2)], 4)
    last_a, last_b = send(to_before, 2, 3), send(to_after, 2, 1)
    near = part(0, [(last_a, 0), (last_b, 0)], 1)
    return gather_sum([near[0]] + [send(near[j], 1, SIDE - j) for j in (1, 2, 3)])


def shards(
    tokens, expert_ids, slot_ids, route_logits, gate_weight, up_weight, down_weight, out_grad
):
    group, z, x, core = (lax.axis_index(a) for a in ("ep", "z", "x", "c"))
    flat = jnp.remainder(expert_ids - group, SIDE) * CAP + slot_ids

    near, far = jnp.arange(16, dtype=jnp.int32) % SIDE, jnp.arange(16, dtype=jnp.int32) // SIDE

    def arrival(c):
        by_z = jnp.where(c == 0, near, far)
        by_x = jnp.where(c == 0, far, near)
        return (
            jnp.remainder(z - by_z, SIDE) * SIDE + jnp.remainder(x - by_x, SIDE)
        ) * 2 + c

    order = jnp.concatenate([arrival(core), arrival(1 - core)]).astype(jnp.int32)

    packed = pack(flat.T, route_logits.T, tokens, out_grad)
    parts = [packed[0]] + [lax.ppermute(packed[j], "ep", ring(j)) for j in (1, 2, 3)]
    own_in, own_grad = assemble(parts)

    gate_rel, up_rel, down_rel = arrange(
        order,
        gate_weight.reshape(BLOCKS, WIDE, HID),
        up_weight.reshape(BLOCKS, WIDE, HID),
        down_weight.reshape(HID, BLOCKS * WIDE),
    )
    down_x, gate_x, up_x = (swap(w[16:]) for w in (down_rel, gate_rel, up_rel))

    in_own = spread(own_in)
    in_other = [swap(p) for p in in_own]
    grad_own = spread(own_grad)
    grad_other = [swap(p) for p in grad_own]

    def contracted(weights, own, other):
        totals = []
        for first, last, index in ((0, 1, 0), (1, 2, 1), (2, 3, 3), (3, 5, 2)):
            totals = contract(weights, own[first:last], other[first:last], totals, index)
        return totals

    gate_act, up_act = contracted([gate_rel, up_rel], in_own, in_other)
    hidden = activate(gate_act, up_act)
    out_rows = reduce([(down_rel, down_x)], (hidden, swap(hidden)), False, "expert_out")

    (hidden_grad,) = contracted([down_rel], grad_own, grad_other)
    rows = differentiate(hidden, gate_act, up_act, hidden_grad)
    back_rows = reduce(
        [(gate_rel, gate_x), (up_rel, up_x)], (rows, swap(rows)), True, "expert_back"
    )

    gate_grad, up_grad = weight_grads(order, in_own, in_other, rows)
    down_grad = down_grads(order, grad_own, grad_other, hidden)

    def returned(blocks):
        return [blocks[0]] + [
            lax.ppermute(blocks[j], "ep", ring(SIDE - j)) for j in (1, 2, 3)
        ]

    mixed = mix(flat, route_logits, returned(out_rows))
    token_grad, logit_grad = collect(flat, route_logits, returned(back_rows))
    return (
        mixed,
        token_grad,
        logit_grad,
        gate_grad.reshape(gate_weight.shape),
        up_grad.reshape(up_weight.shape),
        down_grad.reshape(down_weight.shape),
    )


def solution(mesh):
    tp = ("z", "x", "c")
    fine = Mesh(mesh.devices.reshape(SIDE, SIDE, SIDE, 2), ("ep", *tp))
    return jax.shard_map(
        shards,
        mesh=fine,
        in_specs=(
            P("ep", tp),
            P("ep", None),
            P("ep", None),
            P("ep", None),
            P("ep", None, tp),
            P("ep", None, tp),
            P("ep", tp, None),
            P("ep", tp),
        ),
        out_specs=(
            P("ep", tp),
            P("ep", tp),
            P("ep", None),
            P("ep", None, tp),
            P("ep", None, tp),
            P("ep", tp, None),
        ),
        check_vma=False,
    )
```

```python
import jax
import jax.numpy as jnp
import numpy as np
from jax import lax
from jax.experimental import pallas as pl
from jax.experimental.pallas import tpu as pltpu
from jax.sharding import Mesh, PartitionSpec as P

CAP = 160
SIDE = 4
WIDE = 192
HID = 256
ROWS = SIDE * CAP
BLOCKS = 32
EXTRA = 16
TP = ("z", "x", "c")
BF = jnp.bfloat16
F32 = jnp.float32
VMEM_LIMIT = 20 * 1024 * 1024


def ring(shift):
    return [(i, (i + shift) % SIDE) for i in range(SIDE)]


def plane(phase, shift):
    pairs = []
    for z in range(SIDE):
        for x in range(SIDE):
            for c in range(2):
                along_z = (phase == 1) == (c == 0)
                to_z, to_x = ((z + shift) % SIDE, x) if along_z else (z, (x + shift) % SIDE)
                pairs.append(((z * SIDE + x) * 2 + c, (to_z * SIDE + to_x) * 2 + c))
    return pairs


def send(value, phase, shift):
    return lax.ppermute(value, TP, plane(phase, shift))


def swap(value):
    return lax.ppermute(value, "c", [(0, 1), (1, 0)])


def dot(a, b, dims=((1,), (0,))):
    return lax.dot_general(a, b, (dims, ((), ())), preferred_element_type=F32)


def shape_of(*dims, dtype=BF):
    return jax.ShapeDtypeStruct(dims, dtype)


def fixed(*at):
    return lambda i, order: at


def run(kernel, order, ins, outs, *, steps=1, after=(), scratch=(), flops=0, name):
    def spec(entry):
        if isinstance(entry, tuple):
            return pl.BlockSpec(entry[1], entry[2]), entry[0]
        return pl.BlockSpec(entry.shape, fixed(*(0,) * len(entry.shape))), entry

    in_specs, arrays = zip(*(spec(e) for e in ins))
    out_specs, shapes = zip(*(spec(e) for e in outs))
    count, idle = len(arrays), len(after)

    def body(order_ref, *refs):
        kernel(order_ref, *refs[:count], *refs[count + idle :])

    moved = 0
    for (block, array) in zip((*in_specs, *out_specs), (*arrays, *shapes)):
        size = min(int(np.prod([n or 1 for n in block.block_shape])) * steps, array.size)
        moved += size * array.dtype.itemsize
    return pl.pallas_call(
        body,
        grid_spec=pltpu.PrefetchScalarGridSpec(
            num_scalar_prefetch=1,
            grid=(steps,),
            in_specs=[*in_specs, *[pl.BlockSpec(memory_space=pl.ANY)] * idle],
            out_specs=list(out_specs),
            scratch_shapes=list(scratch),
        ),
        out_shape=list(shapes),
        compiler_params=pltpu.CompilerParams(vmem_limit_bytes=VMEM_LIMIT),
        cost_estimate=pl.CostEstimate(flops=flops, bytes_accessed=moved, transcendentals=0),
        name=name,
    )(order, *arrays, *after)


def choices(flat, logits, j):
    gap = logits[0:1, :] - logits[1:2, :]
    slot = lax.broadcasted_iota(jnp.int32, (CAP, flat.shape[1]), 0) + CAP * j
    first, second = slot == flat[0:1, :], slot == flat[1:2, :]
    weight = jnp.where(first, jax.nn.sigmoid(gap), 0.0) + jnp.where(
        second, jax.nn.sigmoid(-gap), 0.0
    )
    return first, second, weight


def pack(group, experts, slots, logits, tokens, out_grad):
    given = [experts, slots, logits, tokens, out_grad]

    def kernel(group_ref, *refs):
        count = len(given)
        ins, outs, flat_out = refs[:count], refs[count : count + SIDE], refs[count + SIDE]
        experts, slots, logits, tok, grad, sem = refs[count + SIDE + 1 :]
        loads = [
            pltpu.make_async_copy(a, b, sem.at[k])
            for k, (a, b) in enumerate(zip(ins, (experts, slots, logits, tok, grad)))
        ]
        for copy in loads:
            copy.start()
        for copy in loads:
            copy.wait()
        flat = lax.rem(experts[...] + (SIDE - group_ref[0]), SIDE) * CAP + slots[...]
        flat_out[...] = flat
        for j in range(SIDE):
            first, second, weight = choices(flat, logits[...], j)
            pick = jnp.where(first | second, 1.0, 0.0).astype(BF)
            weight = jnp.sum(weight, axis=1, keepdims=True)
            outs[j][:, :WIDE] = dot(pick, tok[...], ((1,), (1,))).astype(BF)
            outs[j][:, WIDE:] = (weight * dot(pick, grad[...], ((1,), (1,)))).astype(BF)

    whole = pl.BlockSpec(memory_space=pltpu.VMEM)
    return pl.pallas_call(
        kernel,
        in_specs=[pl.BlockSpec(memory_space=pltpu.SMEM)]
        + [pl.BlockSpec(memory_space=pl.ANY)] * len(given),
        out_specs=[whole] * (SIDE + 1),
        out_shape=[shape_of(CAP, 2 * WIDE)] * SIDE + [shape_of(*slots.shape, dtype=jnp.int32)],
        scratch_shapes=[pltpu.VMEM(a.shape, a.dtype) for a in given]
        + [pltpu.SemaphoreType.DMA((len(given),))],
        compiler_params=pltpu.CompilerParams(vmem_limit_bytes=62 * 1024 * 1024),
        cost_estimate=pl.CostEstimate(
            flops=4 * ROWS * 256 * WIDE, bytes_accessed=4 * ROWS * WIDE, transcendentals=0
        ),
        name="pack_rows",
    )(group, *given)


def assemble(order, parts):
    def kernel(_, *refs):
        refs[SIDE][...] = jnp.concatenate([r[...] for r in refs[:SIDE]], axis=0).T

    return run(kernel, order, parts, [shape_of(2 * WIDE, ROWS)], name="assemble_columns")[0]


def arrange(order, gate, up, down, after):
    per = 4

    def kernel(order_ref, gate_in, up_in, down_in, gate_out, up_out, own_out, send_out):
        odd = lax.rem(order_ref[0], 2) == 1
        turned = down_in[...].T.reshape(per, 2, WIDE, HID)
        own_out[...] = jnp.where(odd, turned[:, 1], turned[:, 0])
        send_out[...] = jnp.where(odd, turned[:, 0], turned[:, 1])
        gate_out[...] = gate_in[...]
        up_out[...] = up_in[...]

    other = ((per, None, WIDE, HID), lambda i, order: (i, 1 - lax.rem(order[0], 2), 0, 0))
    out = (shape_of(BLOCKS // 2, WIDE, HID), (per, WIDE, HID), lambda i, order: (i, 0, 0))
    return run(
        kernel,
        order,
        [
            (gate.reshape(BLOCKS // 2, 2, WIDE, HID), *other),
            (up.reshape(BLOCKS // 2, 2, WIDE, HID), *other),
            (down, (HID, per * 2 * WIDE), lambda i, order: (0, i)),
        ],
        [out] * 4,
        steps=BLOCKS // 2 // per,
        after=after,
        name="arrange_weights",
    )


def contract(order, weights, chunks, totals, finish=None, after=()):
    steps = 2 * len(chunks)
    pieces, users = [], [[] for _ in range(steps)]
    for k, (_, own, other) in enumerate(chunks):
        for side in (own, other):
            if len(side) == 1:
                at = lambda i, order, k=k: (jnp.clip(i - 2 * k, 0, 1), 0, 0)
                pieces.append((side[0], (2, WIDE, ROWS), at))
                users[2 * k].append(len(pieces) - 1)
                users[2 * k + 1].append(len(pieces) - 1)
            else:
                for half, array in enumerate(side):
                    pieces.append(array)
                    users[2 * k + half].append(len(pieces) - 1)

    def place(i):
        at = chunks[0][0]
        for k in range(1, len(chunks)):
            at = jnp.where(i >= 2 * k, chunks[k][0], at)
        return at * SIDE + lax.rem(i, 2) * 2

    mats = []
    for own, other, divisor in weights:
        for base, array in ((0, own), (16, other)):
            for b in range(2):
                at = lambda i, order, base=base, b=b, divisor=divisor: (
                    order[base + place(i) + b] // divisor,
                    0,
                    0,
                )
                mats.append((array, (None, WIDE, HID), at))
    more = list(finish[1]) if finish else []
    results = list(finish[2]) if finish else [shape_of(HID, ROWS, dtype=F32)] * len(weights)
    cuts = np.cumsum([len(pieces), len(mats), len(totals), len(more), len(results)])

    def kernel(_, *refs):
        p, m, before, given, outs, held = (
            refs[a:b] for a, b in zip([0, *cuts], [*cuts, len(refs)])
        )
        held = held if finish else outs
        for s in range(steps):

            @pl.when(pl.program_id(0) == s)
            def _():
                piece = jnp.concatenate(
                    [p[u][...].reshape(2 * WIDE, ROWS) for u in users[s]], axis=0
                )
                for w in range(len(weights)):
                    mat = jnp.concatenate([r[...] for r in m[4 * w : 4 * w + 4]], axis=0)
                    total = dot(mat, piece, ((0,), (0,)))
                    if s > 0:
                        total += held[w][...]
                    elif totals:
                        total += before[w][...]
                    held[w][...] = total
                if finish and s == steps - 1:
                    finish[0](held, given, outs)

    return run(
        kernel,
        order,
        [*pieces, *mats, *totals, *more],
        results,
        steps=steps,
        after=after,
        scratch=[pltpu.VMEM((HID, ROWS), F32)] * len(weights) if finish else [],
        flops=len(weights) * len(chunks) * 16 * WIDE * HID * ROWS,
        name="contract_features",
    )


def activate(totals, given, outs):
    g, u = totals[0][...], totals[1][...]
    outs[0][...] = g
    outs[1][...] = u
    outs[2][...] = (g * jax.nn.sigmoid(g) * u).astype(BF)


def differentiate(totals, given, outs):
    hidden, gate, up = given
    g, hg = gate[...], totals[0][...]
    s = jax.nn.sigmoid(g)
    outs[0][0:HID] = (hg * up[...] * s * (1.0 + g * (1.0 - s))).astype(BF)
    outs[0][HID : 2 * HID] = (hg * g * s).astype(BF)
    product = hidden[...].astype(F32) * hg
    outs[0][2 * HID :] = jnp.sum(product.reshape(HID // EXTRA, EXTRA, ROWS), axis=0).astype(BF)


def expand(order, weights, acts, places, outs, store, more=(), after=(), *, name):
    pairs = len(weights)
    ins = list(acts)
    for place in places:
        for own, divisor, other in weights:
            for array, by in ((own, divisor), (other, 2)):
                for b in range(SIDE):
                    at = lambda i, order, n=SIDE * place + b, by=by: (order[n] // by, 0, 0)
                    ins.append((array, (None, WIDE, HID), at))
    per = pairs * 2 * SIDE
    first_more = len(ins)
    ins += list(more)

    def kernel(_, own, other, *refs):
        mats = refs[: first_more - 2]
        given = refs[first_more - 2 : first_more - 2 + len(more)]
        results = refs[first_more - 2 + len(more) :]
        act = jnp.concatenate(
            [a[w * HID : (w + 1) * HID] for w in range(pairs) for a in (own, other)], axis=0
        )
        tail = None
        if acts[0].shape[0] > pairs * HID:
            tail = own[pairs * HID :].astype(F32) + other[pairs * HID :].astype(F32)
        for k in range(len(places)):
            for b in range(SIDE):
                block = [mats[k * per + n * SIDE + b][...] for n in range(pairs * 2)]
                value = dot(jnp.concatenate(block, axis=1), act)
                store(k, b, value, tail, given, results)

    return run(
        kernel,
        order,
        ins,
        outs,
        after=after,
        flops=len(places) * pairs * 16 * WIDE * HID * ROWS,
        name=name,
    )


def gather_sum(order, parts):
    both = 2 * WIDE

    def kernel(_, *refs):
        total = sum(r[...].astype(F32) for r in refs[:SIDE])
        rows = total[:both].astype(BF).T
        product = jnp.sum(total[both:], axis=0, keepdims=True)
        high = product.astype(BF)
        low = (product - high.astype(F32)).astype(BF)
        for j in range(SIDE):
            out, cut = refs[SIDE + j], slice(j * CAP, (j + 1) * CAP)
            out[:CAP] = rows[cut]
            line = lax.broadcasted_iota(jnp.int32, (EXTRA, CAP), 0)
            lines = jnp.where(line == 0, high[:, cut].astype(F32), 0.0) + jnp.where(
                line == 1, low[:, cut].astype(F32), 0.0
            )
            out[CAP:, :CAP] = lines.astype(BF)
            out[CAP:, CAP:] = jnp.zeros((EXTRA, both - CAP), BF)

    return run(kernel, order, parts, [shape_of(CAP + EXTRA, both)] * SIDE, name="sum_rows")


def collect(order, flat, logits, parts):
    tokens = flat.shape[1]

    def kernel(_, flat, logits, *refs):
        got, (mixed, back, grads) = refs[:SIDE], refs[SIDE:]
        out, tok, product = 0.0, 0.0, [0.0, 0.0]
        for j in range(SIDE):
            first, second, weight = choices(flat[...], logits[...], j)
            high = weight.astype(BF)
            low = (weight - high.astype(F32)).astype(BF)
            picks = [jnp.where(pick, 1.0, 0.0).astype(BF) for pick in (first, second)]
            cols = got[j][:CAP].T
            out += dot(cols[:WIDE], high) + dot(cols[:WIDE], low)
            tok += dot(cols[WIDE:], picks[0]) + dot(cols[WIDE:], picks[1])
            for k in range(2):
                product[k] += dot(got[j][CAP:, :CAP], picks[k])
        mixed[...] = out.astype(BF)
        back[...] = tok.astype(BF)
        gap = logits[0:1, :] - logits[1:2, :]
        one, two = (jnp.sum(p, axis=0, keepdims=True) for p in product)
        cross = jax.nn.sigmoid(-gap) * one - jax.nn.sigmoid(gap) * two
        grads[...] = jnp.concatenate([cross, -cross], axis=0)

    return run(
        kernel,
        order,
        [flat, logits, *parts],
        [shape_of(WIDE, tokens), shape_of(WIDE, tokens), shape_of(2, tokens, dtype=F32)],
        flops=8 * tokens * ROWS * WIDE,
        name="collect_rows",
    )


PIECES = ((0, 4), (4, 4), (12, 4), (8, 2), (10, 2))
STARTS = [(base + first, n) for base in (0, 16) for first, n in PIECES]


def gradient_call(kernel, order, rows, pieces, outs, scratch, flops, name):
    moved = 2 * BLOCKS * WIDE * (ROWS + HID * len(outs))
    return pl.pallas_call(
        kernel,
        in_specs=[pl.BlockSpec(memory_space=pltpu.SMEM)]
        + [pl.BlockSpec(memory_space=pltpu.VMEM)] * (1 + len(pieces)),
        out_specs=[pl.BlockSpec(memory_space=pl.ANY)] * len(outs),
        out_shape=outs,
        scratch_shapes=scratch,
        compiler_params=pltpu.CompilerParams(vmem_limit_bytes=VMEM_LIMIT),
        cost_estimate=pl.CostEstimate(flops=flops, bytes_accessed=moved, transcendentals=0),
        name=name,
    )(order, rows, *pieces)


def weight_grads(order, pieces, rows):
    def kernel(order_ref, rows_ref, *refs):
        count = len(pieces)
        ins, outs = refs[:count], refs[count : count + 2]
        done, sem = refs[count + 2 :]
        stores = []
        act = rows_ref[: 2 * HID]
        for k, (first, n) in enumerate(STARTS):
            piece = ins[k][...].reshape(n * WIDE, ROWS)
            value = dot(piece, act, ((1,), (1,))).astype(BF).reshape(n, WIDE, 2 * HID)
            for w in range(2):
                done[w, first : first + n] = value[:, :, w * HID : (w + 1) * HID]
                for b in range(first, first + n):
                    stores.append(
                        pltpu.make_async_copy(
                            done.at[w, b], outs[w].at[order_ref[b]], sem.at[w, b]
                        )
                    )
                    stores[-1].start()
        for copy in stores:
            copy.wait()

    return gradient_call(
        kernel,
        order,
        rows,
        pieces,
        [shape_of(BLOCKS, WIDE, HID)] * 2,
        [pltpu.VMEM((2, BLOCKS, WIDE, HID), BF), pltpu.SemaphoreType.DMA((2, BLOCKS))],
        4 * BLOCKS * WIDE * HID * ROWS,
        "weight_gradients",
    )


def down_grads(order, pieces, hidden):
    def kernel(order_ref, hidden_ref, *refs):
        count = len(pieces)
        ins, out = refs[:count], refs[count]
        placed, done, sem = refs[count + 1 :]
        act = hidden_ref[...]
        for k, (first, n) in enumerate(STARTS):
            piece = ins[k][...].reshape(n * WIDE, ROWS)
            value = dot(piece, act, ((1,), (1,))).astype(BF).reshape(n, WIDE, HID)
            for b in range(n):
                placed[order_ref[first + b]] = value[b]
        stores = []
        for s in range(BLOCKS // 2):
            done[s] = placed[2 * s : 2 * s + 2].reshape(2 * WIDE, HID).T
            stores.append(
                pltpu.make_async_copy(
                    done.at[s], out.at[:, pl.ds(s * 2 * WIDE, 2 * WIDE)], sem.at[s]
                )
            )
            stores[-1].start()
        for copy in stores:
            copy.wait()

    return gradient_call(
        kernel,
        order,
        hidden,
        pieces,
        [shape_of(HID, BLOCKS * WIDE)],
        [
            pltpu.VMEM((BLOCKS, WIDE, HID), BF),
            pltpu.VMEM((BLOCKS // 2, HID, 2 * WIDE), BF),
            pltpu.SemaphoreType.DMA((BLOCKS // 2,)),
        ],
        2 * BLOCKS * WIDE * HID * ROWS,
        "down_gradients",
    )[0]


def hold(arrays, after):
    def kernel(*refs):
        pass

    return pl.pallas_call(
        kernel,
        in_specs=[pl.BlockSpec(memory_space=pl.ANY)] * (len(arrays) + len(after)),
        out_specs=[pl.BlockSpec(memory_space=pl.ANY)] * len(arrays),
        out_shape=[jax.ShapeDtypeStruct(a.shape, a.dtype) for a in arrays],
        input_output_aliases={k: k for k in range(len(arrays))},
        compiler_params=pltpu.CompilerParams(vmem_limit_bytes=VMEM_LIMIT),
        cost_estimate=pl.CostEstimate(flops=0, bytes_accessed=0, transcendentals=0),
        name="hold",
    )(*arrays, *after)


def stack(order, blocks, after):
    def kernel(_, *refs):
        for j in range(SIDE):
            refs[SIDE][j] = refs[j][:WIDE]
            refs[SIDE + 1][j] = refs[j][WIDE:]

    return run(
        kernel,
        order,
        blocks,
        [shape_of(SIDE, WIDE, ROWS)] * 2,
        after=after,
        name="stack_blocks",
    )


def halves(order, arrived):
    def kernel(_, from_before, from_after, *outs):
        outs[0][...] = from_before[...]
        outs[1][...] = from_after[...]

    half = (2, WIDE, ROWS)
    return run(
        kernel,
        order,
        [(arrived[0], half, fixed(0, 0, 0)), (arrived[1], half, fixed(1, 0, 0))],
        [shape_of(*half)] * 2,
        name="half_blocks",
    )


def shards(
    tokens, expert_ids, slot_ids, route_logits, gate_weight, up_weight, down_weight, out_grad
):
    group, z, x, core = (lax.axis_index(a) for a in ("ep", "z", "x", "c"))
    logits = route_logits.T

    near, far = jnp.arange(16, dtype=jnp.int32) % SIDE, jnp.arange(16, dtype=jnp.int32) // SIDE

    def arrival(c):
        by_z = jnp.where(c == 0, near, far)
        by_x = jnp.where(c == 0, far, near)
        return (
            jnp.remainder(z - by_z, SIDE) * SIDE + jnp.remainder(x - by_x, SIDE)
        ) * 2 + c

    order = jnp.concatenate([arrival(core), arrival(1 - core)]).astype(jnp.int32)
    gate = gate_weight.reshape(BLOCKS, WIDE, HID)
    up = up_weight.reshape(BLOCKS, WIDE, HID)
    down = down_weight.reshape(HID, BLOCKS * WIDE)

    *packed, flat = pack(
        group.reshape(1), expert_ids.T, slot_ids.T, logits, tokens.T, out_grad.T
    )
    part_2, part_1, part_3 = (lax.ppermute(packed[j], "ep", ring(j)) for j in (2, 1, 3))
    parts = [packed[0], part_1, part_2, part_3]
    own = assemble(order, parts)
    gate_send, up_send, down_own, down_send = arrange(order, gate, up, down, [own])
    gate_x, up_x, down_x = swap(gate_send), swap(up_send), swap(down_send)

    in_weights = [(gate, gate, 1), (up, up, 1)]
    near_in, near_grad = stack(
        order, [own] + [send(own, 1, k) for k in (1, 2, 3)], [gate_send, down_own]
    )
    near_in_x, near_grad_x = swap(near_in), swap(near_grad)
    in_1, in_3 = send(near_in, 2, 1), send(near_in, 2, 3)
    totals = contract(
        order,
        in_weights,
        [(0, [near_in], [near_in_x])],
        [],
        after=[gate_x, up_x, down_x, near_grad_x],
    )
    in_1, in_3 = hold([in_1, in_3], totals)
    in_a, in_b = halves(order, [in_1, in_3])
    in_2 = [send(in_a, 2, 1), send(in_b, 2, 3)]
    in_1x, in_3x = swap(in_1), swap(in_3)
    totals = contract(
        order, in_weights, [(1, [in_1], [in_1x]), (3, [in_3], [in_3x])], totals, after=[in_a]
    )
    in_2 = hold(in_2, totals)
    in_2x = [swap(p) for p in in_2]
    (near_grad,) = hold([near_grad], in_2x)
    grad_1, grad_3 = send(near_grad, 2, 1), send(near_grad, 2, 3)
    wide = shape_of(HID, ROWS, dtype=F32)
    gate_act, up_act, hidden = contract(
        order,
        in_weights,
        [(2, in_2, in_2x)],
        totals,
        (activate, [], [wide, wide, shape_of(HID, ROWS)]),
    )

    acts = (hidden, swap(hidden))
    out_weights = [(down_own, 2, down_x)]
    block4, block2 = shape_of(SIDE, WIDE, ROWS), shape_of(2, WIDE, ROWS)

    def split(k, b, value, tail, given, outs):
        outs[b // 2][b % 2] = value.astype(BF)

    def add_relayed(k, b, value, tail, given, outs):
        if b // 2 == k:
            value += given[k][b % 2].astype(F32)
        outs[k][b] = value.astype(BF)

    def add_last(k, b, value, tail, given, outs):
        outs[0][b] = (value + given[0][b].astype(F32) + given[1][b].astype(F32)).astype(BF)

    out_a, out_b = expand(
        order, out_weights, acts, [2], [block2] * 2, split, name="expert_out"
    )
    relayed = [send(out_a, 2, 3), send(out_b, 2, 1)]

    grad_1, grad_3 = hold([grad_1, grad_3], relayed)
    grad_a, grad_b = halves(order, [grad_1, grad_3])
    grad_2 = [send(grad_a, 2, 1), send(grad_b, 2, 3)]
    grad_1x, grad_3x = swap(grad_1), swap(grad_3)
    grad_weights = [(down_own, down_send, 2)]
    out_1, out_3 = expand(
        order,
        out_weights,
        acts,
        [1, 3],
        [block4] * 2,
        add_relayed,
        relayed,
        [grad_a],
        name="expert_out",
    )
    arrived = [send(out_1, 2, 3), send(out_3, 2, 1)]
    totals = contract(
        order,
        grad_weights,
        [
            (0, [near_grad], [near_grad_x]),
            (1, [grad_1], [grad_1x]),
            (3, [grad_3], [grad_3x]),
        ],
        [],
        after=[out_1],
    )
    grad_2 = hold(grad_2, totals)
    grad_2x = [swap(p) for p in grad_2]
    (rows,) = contract(
        order,
        grad_weights,
        [(2, grad_2, grad_2x)],
        totals,
        (differentiate, [hidden, gate_act, up_act], [shape_of(2 * HID + EXTRA, ROWS)]),
    )
    (near_out,) = expand(
        order, out_weights, acts, [0], [block4], add_last, arrived, name="expert_out"
    )

    acts = (rows, swap(rows))
    back_weights = [(gate, 1, gate_x), (up, 1, up_x)]
    tall = WIDE + EXTRA

    def plain(k, b, value, tail, given, outs):
        outs[k][b, :WIDE] = value.astype(BF)
        outs[k][b, WIDE:] = tail.astype(BF)

    def join(k, b, value, tail, given, outs):
        outs[b][:WIDE] = given[3][b]
        for ref in given[:3]:
            value += ref[b, :WIDE].astype(F32)
            tail = tail + ref[b, WIDE:].astype(F32)
        outs[b][WIDE : 2 * WIDE] = value.astype(BF)
        outs[b][2 * WIDE :] = tail.astype(BF)

    block = shape_of(SIDE, tall, ROWS)
    (back_2,) = expand(
        order, back_weights, acts, [2], [block], plain, [], [near_out], name="expert_back"
    )
    back_1, back_3 = expand(
        order, back_weights, acts, [1, 3], [block] * 2, plain, [], [back_2], name="expert_back"
    )
    arrived = [send(back_2, 2, 2), send(back_1, 2, 3), send(back_3, 2, 1)]
    gate_grad, up_grad = weight_grads(
        order, [near_in, in_1, in_3, *in_2, near_in_x, in_1x, in_3x, *in_2x], rows
    )
    down_grad = down_grads(
        order,
        [near_grad, grad_1, grad_3, *grad_2, near_grad_x, grad_1x, grad_3x, *grad_2x],
        hidden,
    )
    sums = expand(
        order,
        back_weights,
        acts,
        [0],
        [shape_of(WIDE + tall, ROWS)] * SIDE,
        join,
        [*arrived, near_out],
        [gate_grad, down_grad],
        name="expert_back",
    )

    sums = gather_sum(order, [sums[0]] + [send(sums[j], 1, SIDE - j) for j in (1, 2, 3)])
    back = [sums[0]] + [lax.ppermute(sums[j], "ep", ring(SIDE - j)) for j in (1, 2, 3)]
    mixed, token_grad, logit_grad = collect(order, flat, logits, back)
    return (
        mixed.T,
        token_grad.T,
        logit_grad.T,
        gate_grad.reshape(gate_weight.shape),
        up_grad.reshape(up_weight.shape),
        down_grad.reshape(down_weight.shape),
    )


def solution(mesh):
    tp = ("z", "x", "c")
    fine = Mesh(mesh.devices.reshape(SIDE, SIDE, SIDE, 2), ("ep", *tp))
    return jax.shard_map(
        shards,
        mesh=fine,
        in_specs=(
            P("ep", tp),
            P("ep", None),
            P("ep", None),
            P("ep", None),
            P("ep", None, tp),
            P("ep", None, tp),
            P("ep", tp, None),
            P("ep", tp),
        ),
        out_specs=(
            P("ep", tp),
            P("ep", tp),
            P("ep", None),
            P("ep", None, tp),
            P("ep", None, tp),
            P("ep", tp, None),
        ),
        check_vma=False,
    )
```

```python
import jax
import jax.numpy as jnp
import numpy as np
from jax import lax
from jax.experimental import pallas as pl
from jax.experimental.pallas import tpu as pltpu
from jax.sharding import Mesh, PartitionSpec as P

CAP = 160
SIDE = 4
WIDE = 192
HID = 256
ROWS = SIDE * CAP
BLOCKS = 32
EXTRA = 16
TP = ("z", "x", "c")
BF = jnp.bfloat16
F32 = jnp.float32
VMEM_LIMIT = 20 * 1024 * 1024


def ring(shift):
    return [(i, (i + shift) % SIDE) for i in range(SIDE)]


def plane(phase, shift):
    pairs = []
    for z in range(SIDE):
        for x in range(SIDE):
            for c in range(2):
                along_z = (phase == 1) == (c == 0)
                to_z, to_x = ((z + shift) % SIDE, x) if along_z else (z, (x + shift) % SIDE)
                pairs.append(((z * SIDE + x) * 2 + c, (to_z * SIDE + to_x) * 2 + c))
    return pairs


def send(value, phase, shift):
    return lax.ppermute(value, TP, plane(phase, shift))


def swap(value):
    return lax.ppermute(value, "c", [(0, 1), (1, 0)])


def dot(a, b, dims=((1,), (0,))):
    return lax.dot_general(a, b, (dims, ((), ())), preferred_element_type=F32)


def shape_of(*dims, dtype=BF):
    return jax.ShapeDtypeStruct(dims, dtype)


def fixed(*at):
    return lambda i, order: at


def run(kernel, order, ins, outs, *, steps=1, after=(), scratch=(), flops=0, name):
    def spec(entry):
        if isinstance(entry, tuple):
            return pl.BlockSpec(entry[1], entry[2]), entry[0]
        return pl.BlockSpec(entry.shape, fixed(*(0,) * len(entry.shape))), entry

    in_specs, arrays = zip(*(spec(e) for e in ins))
    out_specs, shapes = zip(*(spec(e) for e in outs))
    count, idle = len(arrays), len(after)

    def body(order_ref, *refs):
        kernel(order_ref, *refs[:count], *refs[count + idle :])

    moved = 0
    for (block, array) in zip((*in_specs, *out_specs), (*arrays, *shapes)):
        size = min(int(np.prod([n or 1 for n in block.block_shape])) * steps, array.size)
        moved += size * array.dtype.itemsize
    return pl.pallas_call(
        body,
        grid_spec=pltpu.PrefetchScalarGridSpec(
            num_scalar_prefetch=1,
            grid=(steps,),
            in_specs=[*in_specs, *[pl.BlockSpec(memory_space=pl.ANY)] * idle],
            out_specs=list(out_specs),
            scratch_shapes=list(scratch),
        ),
        out_shape=list(shapes),
        compiler_params=pltpu.CompilerParams(vmem_limit_bytes=VMEM_LIMIT),
        cost_estimate=pl.CostEstimate(flops=flops, bytes_accessed=moved, transcendentals=0),
        name=name,
    )(order, *arrays, *after)


def choices(flat, logits, j):
    gap = logits[0:1, :] - logits[1:2, :]
    slot = lax.broadcasted_iota(jnp.int32, (CAP, flat.shape[1]), 0) + CAP * j
    first, second = slot == flat[0:1, :], slot == flat[1:2, :]
    weight = jnp.where(first, jax.nn.sigmoid(gap), 0.0) + jnp.where(
        second, jax.nn.sigmoid(-gap), 0.0
    )
    return first, second, weight


def pack(group, experts, slots, logits, tokens, out_grad):
    given = [experts, slots, logits, tokens, out_grad]

    def kernel(group_ref, *refs):
        count = len(given)
        ins, outs, flat_out = refs[:count], refs[count : count + SIDE], refs[count + SIDE]
        experts, slots, logits, tok, grad, sem = refs[count + SIDE + 1 :]
        loads = [
            pltpu.make_async_copy(a, b, sem.at[k])
            for k, (a, b) in enumerate(zip(ins, (experts, slots, logits, tok, grad)))
        ]
        for copy in loads:
            copy.start()
        for copy in loads:
            copy.wait()
        flat = lax.rem(experts[...] + (SIDE - group_ref[0]), SIDE) * CAP + slots[...]
        flat_out[...] = flat
        for j in range(SIDE):
            first, second, weight = choices(flat, logits[...], j)
            pick = jnp.where(first | second, 1.0, 0.0).astype(BF)
            weight = jnp.sum(weight, axis=1, keepdims=True)
            outs[j][:, :WIDE] = dot(pick, tok[...], ((1,), (1,))).astype(BF)
            outs[j][:, WIDE:] = (weight * dot(pick, grad[...], ((1,), (1,)))).astype(BF)

    whole = pl.BlockSpec(memory_space=pltpu.VMEM)
    return pl.pallas_call(
        kernel,
        in_specs=[pl.BlockSpec(memory_space=pltpu.SMEM)]
        + [pl.BlockSpec(memory_space=pl.ANY)] * len(given),
        out_specs=[whole] * (SIDE + 1),
        out_shape=[shape_of(CAP, 2 * WIDE)] * SIDE + [shape_of(*slots.shape, dtype=jnp.int32)],
        scratch_shapes=[pltpu.VMEM(a.shape, a.dtype) for a in given]
        + [pltpu.SemaphoreType.DMA((len(given),))],
        compiler_params=pltpu.CompilerParams(vmem_limit_bytes=62 * 1024 * 1024),
        cost_estimate=pl.CostEstimate(
            flops=4 * ROWS * 256 * WIDE, bytes_accessed=4 * ROWS * WIDE, transcendentals=0
        ),
        name="pack_rows",
    )(group, *given)


def assemble(order, parts):
    def kernel(_, *refs):
        cols = jnp.concatenate([r[...] for r in refs[:SIDE]], axis=0).T
        refs[SIDE][...] = cols[:WIDE]
        refs[SIDE + 1][...] = cols[WIDE:]

    return run(kernel, order, parts, [shape_of(WIDE, ROWS)] * 2, name="assemble_columns")


def arrange(order, gate, up, down, after):
    per = 4

    def kernel(order_ref, gate_in, up_in, down_in, gate_out, up_out, own_out, send_out):
        odd = lax.rem(order_ref[0], 2) == 1
        turned = down_in[...].T.reshape(per, 2, WIDE, HID)
        own_out[...] = jnp.where(odd, turned[:, 1], turned[:, 0])
        send_out[...] = jnp.where(odd, turned[:, 0], turned[:, 1])
        gate_out[...] = gate_in[...]
        up_out[...] = up_in[...]

    other = ((per, None, WIDE, HID), lambda i, order: (i, 1 - lax.rem(order[0], 2), 0, 0))
    out = (shape_of(BLOCKS // 2, WIDE, HID), (per, WIDE, HID), lambda i, order: (i, 0, 0))
    return run(
        kernel,
        order,
        [
            (gate.reshape(BLOCKS // 2, 2, WIDE, HID), *other),
            (up.reshape(BLOCKS // 2, 2, WIDE, HID), *other),
            (down, (HID, per * 2 * WIDE), lambda i, order: (0, i)),
        ],
        [out] * 4,
        steps=BLOCKS // 2 // per,
        after=after,
        name="arrange_weights",
    )


def contract(order, weights, chunks, totals, finish=None, after=()):
    steps = 2 * len(chunks)
    pieces, users = [], [[] for _ in range(steps)]
    for k, (_, own, other) in enumerate(chunks):
        for side in (own, other):
            if len(side) == 1:
                at = lambda i, order, k=k: (jnp.clip(i - 2 * k, 0, 1), 0, 0)
                pieces.append((side[0], (2, WIDE, ROWS), at))
                users[2 * k].append(len(pieces) - 1)
                users[2 * k + 1].append(len(pieces) - 1)
            else:
                for half, array in enumerate(side):
                    pieces.append(array)
                    users[2 * k + half].append(len(pieces) - 1)

    def place(i):
        at = chunks[0][0]
        for k in range(1, len(chunks)):
            at = jnp.where(i >= 2 * k, chunks[k][0], at)
        return at * SIDE + lax.rem(i, 2) * 2

    mats = []
    for own, other, divisor in weights:
        for base, array in ((0, own), (16, other)):
            for b in range(2):
                at = lambda i, order, base=base, b=b, divisor=divisor: (
                    order[base + place(i) + b] // divisor,
                    0,
                    0,
                )
                mats.append((array, (None, WIDE, HID), at))
    more = list(finish[1]) if finish else []
    results = list(finish[2]) if finish else [shape_of(HID, ROWS, dtype=F32)] * len(weights)
    cuts = np.cumsum([len(pieces), len(mats), len(totals), len(more), len(results)])

    def kernel(_, *refs):
        p, m, before, given, outs, held = (
            refs[a:b] for a, b in zip([0, *cuts], [*cuts, len(refs)])
        )
        held = held if finish else outs
        for s in range(steps):

            @pl.when(pl.program_id(0) == s)
            def _():
                piece = jnp.concatenate(
                    [p[u][...].reshape(2 * WIDE, ROWS) for u in users[s]], axis=0
                )
                for w in range(len(weights)):
                    mat = jnp.concatenate([r[...] for r in m[4 * w : 4 * w + 4]], axis=0)
                    total = dot(mat, piece, ((0,), (0,)))
                    if s > 0:
                        total += held[w][...]
                    elif totals:
                        total += before[w][...]
                    held[w][...] = total
                if finish and s == steps - 1:
                    finish[0](held, given, outs)

    return run(
        kernel,
        order,
        [*pieces, *mats, *totals, *more],
        results,
        steps=steps,
        after=after,
        scratch=[pltpu.VMEM((HID, ROWS), F32)] * len(weights) if finish else [],
        flops=len(weights) * len(chunks) * 16 * WIDE * HID * ROWS,
        name="contract_features",
    )


def activate(totals, given, outs):
    g, u = totals[0][...], totals[1][...]
    outs[0][...] = g
    outs[1][...] = u
    outs[2][...] = (g * jax.nn.sigmoid(g) * u).astype(BF)


def differentiate(totals, given, outs):
    hidden, gate, up = given
    g, hg = gate[...], totals[0][...]
    s = jax.nn.sigmoid(g)
    outs[0][0:HID] = (hg * up[...] * s * (1.0 + g * (1.0 - s))).astype(BF)
    outs[0][HID : 2 * HID] = (hg * g * s).astype(BF)
    product = hidden[...].astype(F32) * hg
    outs[0][2 * HID :] = jnp.sum(product.reshape(HID // EXTRA, EXTRA, ROWS), axis=0).astype(BF)


def expand(order, weights, acts, places, outs, store, more=(), after=(), *, name):
    pairs = len(weights)
    ins = list(acts)
    for place in places:
        for own, divisor, other in weights:
            for array, by in ((own, divisor), (other, 2)):
                for b in range(SIDE):
                    at = lambda i, order, n=SIDE * place + b, by=by: (order[n] // by, 0, 0)
                    ins.append((array, (None, WIDE, HID), at))
    per = pairs * 2 * SIDE
    first_more = len(ins)
    ins += list(more)

    def kernel(_, own, other, *refs):
        mats = refs[: first_more - 2]
        given = refs[first_more - 2 : first_more - 2 + len(more)]
        results = refs[first_more - 2 + len(more) :]
        act = jnp.concatenate(
            [a[w * HID : (w + 1) * HID] for w in range(pairs) for a in (own, other)], axis=0
        )
        tail = None
        if acts[0].shape[0] > pairs * HID:
            tail = own[pairs * HID :].astype(F32) + other[pairs * HID :].astype(F32)
        for k in range(len(places)):
            for b in range(SIDE):
                block = [mats[k * per + n * SIDE + b][...] for n in range(pairs * 2)]
                value = dot(jnp.concatenate(block, axis=1), act)
                store(k, b, value, tail, given, results)

    return run(
        kernel,
        order,
        ins,
        outs,
        after=after,
        flops=len(places) * pairs * 16 * WIDE * HID * ROWS,
        name=name,
    )


def combine(order, near_out, back):
    def kernel(_, near, *refs):
        for b in range(SIDE):
            total = sum(r[b].astype(F32) for r in refs[:SIDE])
            refs[SIDE + b][:WIDE] = near[b]
            refs[SIDE + b][WIDE:] = total.astype(BF)

    outs = [shape_of(2 * WIDE + EXTRA, ROWS)] * SIDE
    return run(kernel, order, [near_out, *back], outs, name="combine_blocks")


def gather_sum(order, parts):
    both = 2 * WIDE

    def kernel(_, *refs):
        total = sum(r[...].astype(F32) for r in refs[:SIDE])
        rows = total[:both].astype(BF).T
        product = jnp.sum(total[both:], axis=0, keepdims=True)
        high = product.astype(BF)
        low = (product - high.astype(F32)).astype(BF)
        for j in range(SIDE):
            out, cut = refs[SIDE + j], slice(j * CAP, (j + 1) * CAP)
            out[:CAP] = rows[cut]
            line = lax.broadcasted_iota(jnp.int32, (EXTRA, CAP), 0)
            lines = jnp.where(line == 0, high[:, cut].astype(F32), 0.0) + jnp.where(
                line == 1, low[:, cut].astype(F32), 0.0
            )
            out[CAP:, :CAP] = lines.astype(BF)
            out[CAP:, CAP:] = jnp.zeros((EXTRA, both - CAP), BF)

    return run(kernel, order, parts, [shape_of(CAP + EXTRA, both)] * SIDE, name="sum_rows")


def collect(order, flat, logits, parts):
    tokens = flat.shape[1]

    def kernel(_, flat, logits, *refs):
        got, (mixed, back, grads) = refs[:SIDE], refs[SIDE:]
        out, tok, product = 0.0, 0.0, [0.0, 0.0]
        for j in range(SIDE):
            first, second, weight = choices(flat[...], logits[...], j)
            high = weight.astype(BF)
            low = (weight - high.astype(F32)).astype(BF)
            picks = [jnp.where(pick, 1.0, 0.0).astype(BF) for pick in (first, second)]
            cols = got[j][:CAP].T
            out += dot(cols[:WIDE], high) + dot(cols[:WIDE], low)
            tok += dot(cols[WIDE:], picks[0]) + dot(cols[WIDE:], picks[1])
            for k in range(2):
                product[k] += dot(got[j][CAP:, :CAP], picks[k])
        mixed[...] = out.astype(BF)
        back[...] = tok.astype(BF)
        gap = logits[0:1, :] - logits[1:2, :]
        one, two = (jnp.sum(p, axis=0, keepdims=True) for p in product)
        cross = jax.nn.sigmoid(-gap) * one - jax.nn.sigmoid(gap) * two
        grads[...] = jnp.concatenate([cross, -cross], axis=0)

    return run(
        kernel,
        order,
        [flat, logits, *parts],
        [shape_of(WIDE, tokens), shape_of(WIDE, tokens), shape_of(2, tokens, dtype=F32)],
        flops=8 * tokens * ROWS * WIDE,
        name="collect_rows",
    )


PIECES = ((0, 4), (4, 4), (12, 4), (8, 4))
STARTS = [(base + first, n) for base in (0, 16) for first, n in PIECES]


def gradient_call(kernel, order, rows, pieces, outs, scratch, flops, name):
    moved = 2 * BLOCKS * WIDE * (ROWS + HID * len(outs))
    return pl.pallas_call(
        kernel,
        in_specs=[pl.BlockSpec(memory_space=pltpu.SMEM)]
        + [pl.BlockSpec(memory_space=pltpu.VMEM)] * (1 + len(pieces)),
        out_specs=[pl.BlockSpec(memory_space=pltpu.HBM)] * len(outs)
        + [pl.BlockSpec(memory_space=pltpu.VMEM)],
        out_shape=[*outs, shape_of(8, 128, dtype=F32)],
        scratch_shapes=scratch,
        compiler_params=pltpu.CompilerParams(vmem_limit_bytes=VMEM_LIMIT),
        cost_estimate=pl.CostEstimate(flops=flops, bytes_accessed=moved, transcendentals=0),
        name=name,
    )(order, rows, *pieces)


def weight_grads(order, pieces, rows):
    def kernel(order_ref, rows_ref, *refs):
        count = len(pieces)
        ins, outs, mark = refs[:count], refs[count : count + 2], refs[count + 2]
        done, sem = refs[count + 3 :]
        mark[...] = jnp.zeros(mark.shape, F32)
        stores = []
        act = rows_ref[: 2 * HID]
        for k, (first, n) in enumerate(STARTS):
            piece = ins[k][...].reshape(n * WIDE, ROWS)
            value = dot(piece, act, ((1,), (1,))).astype(BF).reshape(n, WIDE, 2 * HID)
            for w in range(2):
                done[w, first : first + n] = value[:, :, w * HID : (w + 1) * HID]
                for b in range(first, first + n):
                    stores.append(
                        pltpu.make_async_copy(
                            done.at[w, b], outs[w].at[order_ref[b]], sem.at[w, b]
                        )
                    )
                    stores[-1].start()
        for copy in stores:
            copy.wait()

    return gradient_call(
        kernel,
        order,
        rows,
        pieces,
        [shape_of(BLOCKS, WIDE, HID)] * 2,
        [pltpu.VMEM((2, BLOCKS, WIDE, HID), BF), pltpu.SemaphoreType.DMA((2, BLOCKS))],
        4 * BLOCKS * WIDE * HID * ROWS,
        "weight_gradients",
    )


def down_grads(order, pieces, hidden):
    def kernel(order_ref, hidden_ref, *refs):
        count = len(pieces)
        ins, out, mark = refs[:count], refs[count], refs[count + 1]
        placed, done, sem = refs[count + 2 :]
        mark[...] = jnp.zeros(mark.shape, F32)
        act = hidden_ref[...]
        for k, (first, n) in enumerate(STARTS):
            piece = ins[k][...].reshape(n * WIDE, ROWS)
            value = dot(piece, act, ((1,), (1,))).astype(BF).reshape(n, WIDE, HID)
            for b in range(n):
                placed[order_ref[first + b]] = value[b]
        stores = []
        for s in range(BLOCKS // 2):
            done[s] = placed[2 * s : 2 * s + 2].reshape(2 * WIDE, HID).T
            stores.append(
                pltpu.make_async_copy(
                    done.at[s], out.at[:, pl.ds(s * 2 * WIDE, 2 * WIDE)], sem.at[s]
                )
            )
            stores[-1].start()
        for copy in stores:
            copy.wait()

    return gradient_call(
        kernel,
        order,
        hidden,
        pieces,
        [shape_of(HID, BLOCKS * WIDE)],
        [
            pltpu.VMEM((BLOCKS, WIDE, HID), BF),
            pltpu.VMEM((BLOCKS // 2, HID, 2 * WIDE), BF),
            pltpu.SemaphoreType.DMA((BLOCKS // 2,)),
        ],
        2 * BLOCKS * WIDE * HID * ROWS,
        "down_gradients",
    )


def hold(arrays, after):
    def kernel(*refs):
        pass

    return pl.pallas_call(
        kernel,
        in_specs=[pl.BlockSpec(memory_space=pl.ANY)] * (len(arrays) + len(after)),
        out_specs=[pl.BlockSpec(memory_space=pl.ANY)] * len(arrays),
        out_shape=[jax.ShapeDtypeStruct(a.shape, a.dtype) for a in arrays],
        input_output_aliases={k: k for k in range(len(arrays))},
        compiler_params=pltpu.CompilerParams(vmem_limit_bytes=VMEM_LIMIT),
        cost_estimate=pl.CostEstimate(flops=0, bytes_accessed=0, transcendentals=0),
        name="hold",
    )(*arrays, *after)


def stack(order, blocks, after):
    def kernel(_, *refs):
        for j in range(SIDE):
            refs[SIDE][j] = refs[j][...]

    outs = [shape_of(SIDE, WIDE, ROWS)]
    return run(kernel, order, blocks, outs, after=after, name="stack_blocks")[0]


def join(order, far, after):
    def kernel(_, first, second, out):
        out[0:2] = first[...]
        out[2:4] = second[...]

    outs = [shape_of(SIDE, WIDE, ROWS)]
    return run(kernel, order, far, outs, after=after, name="join_blocks")[0]


def halves(order, arrived, after=()):
    def kernel(_, from_before, from_after, *outs):
        outs[0][...] = from_before[...]
        outs[1][...] = from_after[...]

    half = (2, WIDE, ROWS)
    return run(
        kernel,
        order,
        [(arrived[0], half, fixed(0, 0, 0)), (arrived[1], half, fixed(1, 0, 0))],
        [shape_of(*half)] * 2,
        after=after,
        name="half_blocks",
    )


def shards(
    tokens, expert_ids, slot_ids, route_logits, gate_weight, up_weight, down_weight, out_grad
):
    group, z, x, core = (lax.axis_index(a) for a in ("ep", "z", "x", "c"))
    logits = route_logits.T

    near, far = jnp.arange(16, dtype=jnp.int32) % SIDE, jnp.arange(16, dtype=jnp.int32) // SIDE

    def arrival(c):
        by_z = jnp.where(c == 0, near, far)
        by_x = jnp.where(c == 0, far, near)
        return (
            jnp.remainder(z - by_z, SIDE) * SIDE + jnp.remainder(x - by_x, SIDE)
        ) * 2 + c

    order = jnp.concatenate([arrival(core), arrival(1 - core)]).astype(jnp.int32)
    gate = gate_weight.reshape(BLOCKS, WIDE, HID)
    up = up_weight.reshape(BLOCKS, WIDE, HID)
    down = down_weight.reshape(HID, BLOCKS * WIDE)

    *packed, flat = pack(
        group.reshape(1), expert_ids.T, slot_ids.T, logits, tokens.T, out_grad.T
    )
    part_2, part_1, part_3 = (lax.ppermute(packed[j], "ep", ring(j)) for j in (2, 1, 3))
    parts = [packed[0], part_1, part_2, part_3]
    own_in, own_grad = assemble(order, parts)

    in_weights = [(gate, gate, 1), (up, up, 1)]
    first = [send(own_in, 1, k) for k in (1, 2, 3)]
    near_in = stack(order, [own_in, *first], [])
    gate_send, up_send, down_own, down_send = arrange(order, gate, up, down, [near_in])
    gate_x, up_x, down_x = swap(gate_send), swap(up_send), swap(down_send)
    first = [send(own_grad, 1, k) for k in (1, 2, 3)]
    near_grad = stack(order, [own_grad, *first], [near_in])
    near_in_x, near_grad_x = swap(near_in), swap(near_grad)
    in_1, in_3 = send(near_in, 2, 1), send(near_in, 2, 3)
    totals = contract(
        order,
        in_weights,
        [(0, [near_in], [near_in_x])],
        [],
        after=[gate_send, down_send, near_grad_x],
    )
    in_1, in_3 = hold([in_1, in_3], totals)
    in_a, in_b = halves(order, [in_1, in_3])
    in_2 = [send(in_a, 2, 1), send(in_b, 2, 3)]
    in_1x, in_3x = swap(in_1), swap(in_3)
    totals = contract(
        order, in_weights, [(1, [in_1], [in_1x]), (3, [in_3], [in_3x])], totals, after=[in_a, gate_x, up_x, down_x]
    )
    (near_grad,) = hold([near_grad], totals)
    grad_1, grad_3 = send(near_grad, 2, 1), send(near_grad, 2, 3)
    in_2 = join(order, in_2, totals)
    in_2x = swap(in_2)
    wide = shape_of(HID, ROWS, dtype=F32)
    gate_act, up_act, hidden = contract(
        order,
        in_weights,
        [(2, [in_2], [in_2x])],
        totals,
        (activate, [], [wide, wide, shape_of(HID, ROWS)]),
    )

    acts = (hidden, swap(hidden))
    out_weights = [(down_own, 2, down_x)]
    block4, block2 = shape_of(SIDE, WIDE, ROWS), shape_of(2, WIDE, ROWS)

    def split(k, b, value, tail, given, outs):
        outs[b // 2][b % 2] = value.astype(BF)

    def add_relayed(k, b, value, tail, given, outs):
        if b // 2 == k:
            value += given[k][b % 2].astype(F32)
        outs[k][b] = value.astype(BF)

    def add_last(k, b, value, tail, given, outs):
        outs[0][b] = (value + given[0][b].astype(F32) + given[1][b].astype(F32)).astype(BF)

    out_a, out_b = expand(
        order, out_weights, acts, [2], [block2] * 2, split, name="expert_out"
    )
    relayed = [send(out_a, 2, 3), send(out_b, 2, 1)]

    grad_1, grad_3 = hold([grad_1, grad_3], relayed)
    grad_a, grad_b = halves(order, [grad_1, grad_3])
    grad_2 = [send(grad_a, 2, 1), send(grad_b, 2, 3)]
    grad_1x, grad_3x = swap(grad_1), swap(grad_3)
    grad_weights = [(down_own, down_send, 2)]
    totals_grad = contract(
        order,
        grad_weights,
        [
            (0, [near_grad], [near_grad_x]),
            (1, [grad_1], [grad_1x]),
            (3, [grad_3], [grad_3x]),
        ],
        [],
        after=[grad_a],
    )

    out_1, out_3 = expand(
        order,
        out_weights,
        acts,
        [1, 3],
        [block4] * 2,
        add_relayed,
        relayed,
        name="expert_out",
    )
    arrived_out = [send(out_1, 2, 3), send(out_3, 2, 1)]
    grad_2 = join(order, grad_2, totals_grad)
    grad_2x = swap(grad_2)
    (rows,) = contract(
        order,
        grad_weights,
        [(2, [grad_2], [grad_2x])],
        totals_grad,
        (differentiate, [hidden, gate_act, up_act], [shape_of(2 * HID + EXTRA, ROWS)]),
        after=[out_1],
    )
    out_acts = acts
    acts = (rows, swap(rows))
    back_weights = [(gate, 1, gate_x), (up, 1, up_x)]
    tall = WIDE + EXTRA

    def plain(k, b, value, tail, given, outs):
        outs[k][b, :WIDE] = value.astype(BF)
        outs[k][b, WIDE:] = tail.astype(BF)

    block = shape_of(SIDE, tall, ROWS)
    (back_2,) = expand(
        order, back_weights, acts, [2], [block], plain, name="expert_back"
    )
    back_1, back_3 = expand(
        order,
        back_weights,
        acts,
        [1, 3],
        [block] * 2,
        plain,
        [],
        [back_2],
        name="expert_back",
    )
    arrived = [send(back_2, 2, 2), send(back_1, 2, 3), send(back_3, 2, 1)]
    (back_0,) = expand(
        order, back_weights, acts, [0], [block], plain, [], [back_1], name="expert_back"
    )
    down_grad, done = down_grads(
        order,
        [near_grad, grad_1, grad_3, grad_2, near_grad_x, grad_1x, grad_3x, grad_2x],
        hold([hidden], [back_0])[0],
    )
    (near_out,) = expand(
        order,
        out_weights,
        out_acts,
        [0],
        [block4],
        add_last,
        arrived_out,
        [done],
        name="expert_out",
    )
    gate_grad, up_grad, done = weight_grads(
        order,
        [near_in, in_1, in_3, in_2, near_in_x, in_1x, in_3x, in_2x],
        hold([rows], [near_out])[0],
    )
    arrived = hold(arrived, [done])
    sums = combine(order, near_out, [back_0, *arrived])

    sums = gather_sum(order, [sums[0]] + [send(sums[j], 1, SIDE - j) for j in (1, 2, 3)])
    back = [sums[0]] + [lax.ppermute(sums[j], "ep", ring(SIDE - j)) for j in (1, 2, 3)]
    mixed, token_grad, logit_grad = collect(order, flat, logits, back)
    return (
        mixed.T,
        token_grad.T,
        logit_grad.T,
        gate_grad.reshape(gate_weight.shape),
        up_grad.reshape(up_weight.shape),
        down_grad.reshape(down_weight.shape),
    )


def solution(mesh):
    tp = ("z", "x", "c")
    fine = Mesh(mesh.devices.reshape(SIDE, SIDE, SIDE, 2), ("ep", *tp))
    return jax.shard_map(
        shards,
        mesh=fine,
        in_specs=(
            P("ep", tp),
            P("ep", None),
            P("ep", None),
            P("ep", None),
            P("ep", None, tp),
            P("ep", None, tp),
            P("ep", tp, None),
            P("ep", tp),
        ),
        out_specs=(
            P("ep", tp),
            P("ep", tp),
            P("ep", None),
            P("ep", None, tp),
            P("ep", None, tp),
            P("ep", tp, None),
        ),
        check_vma=False,
    )
```

```python
import jax
import jax.numpy as jnp
import numpy as np
from jax import lax
from jax.experimental import pallas as pl
from jax.experimental.pallas import tpu as pltpu
from jax.sharding import Mesh, PartitionSpec as P

CAP = 160
SIDE = 4
WIDE = 192
HID = 256
ROWS = SIDE * CAP
BLOCKS = 32
EXTRA = 16
TP = ("z", "x", "c")
BF = jnp.bfloat16
F32 = jnp.float32
VMEM_LIMIT = 20 * 1024 * 1024


def ring(shift):
    return [(i, (i + shift) % SIDE) for i in range(SIDE)]


def plane(phase, shift):
    pairs = []
    for z in range(SIDE):
        for x in range(SIDE):
            for c in range(2):
                along_z = (phase == 1) == (c == 0)
                to_z, to_x = ((z + shift) % SIDE, x) if along_z else (z, (x + shift) % SIDE)
                pairs.append(((z * SIDE + x) * 2 + c, (to_z * SIDE + to_x) * 2 + c))
    return pairs


def send(value, phase, shift):
    return lax.ppermute(value, TP, plane(phase, shift))


def swap(value):
    return lax.ppermute(value, "c", [(0, 1), (1, 0)])


def dot(a, b, dims=((1,), (0,))):
    return lax.dot_general(a, b, (dims, ((), ())), preferred_element_type=F32)


def shape_of(*dims, dtype=BF):
    return jax.ShapeDtypeStruct(dims, dtype)


def fixed(*at):
    return lambda i, order: at


def run(kernel, order, ins, outs, *, steps=1, after=(), scratch=(), flops=0, name):
    def spec(entry):
        if isinstance(entry, tuple):
            return pl.BlockSpec(entry[1], entry[2]), entry[0]
        return pl.BlockSpec(entry.shape, fixed(*(0,) * len(entry.shape))), entry

    in_specs, arrays = zip(*(spec(e) for e in ins))
    out_specs, shapes = zip(*(spec(e) for e in outs))
    count, idle = len(arrays), len(after)

    def body(order_ref, *refs):
        kernel(order_ref, *refs[:count], *refs[count + idle :])

    moved = 0
    for (block, array) in zip((*in_specs, *out_specs), (*arrays, *shapes)):
        size = min(int(np.prod([n or 1 for n in block.block_shape])) * steps, array.size)
        moved += size * array.dtype.itemsize
    return pl.pallas_call(
        body,
        grid_spec=pltpu.PrefetchScalarGridSpec(
            num_scalar_prefetch=1,
            grid=(steps,),
            in_specs=[*in_specs, *[pl.BlockSpec(memory_space=pl.ANY)] * idle],
            out_specs=list(out_specs),
            scratch_shapes=list(scratch),
        ),
        out_shape=list(shapes),
        compiler_params=pltpu.CompilerParams(vmem_limit_bytes=VMEM_LIMIT),
        cost_estimate=pl.CostEstimate(flops=flops, bytes_accessed=moved, transcendentals=0),
        name=name,
    )(order, *arrays, *after)


def choices(flat, logits, j):
    gap = logits[0:1, :] - logits[1:2, :]
    slot = lax.broadcasted_iota(jnp.int32, (CAP, flat.shape[1]), 0) + CAP * j
    first, second = slot == flat[0:1, :], slot == flat[1:2, :]
    weight = jnp.where(first, jax.nn.sigmoid(gap), 0.0) + jnp.where(
        second, jax.nn.sigmoid(-gap), 0.0
    )
    return first, second, weight


def pack(group, experts, slots, logits, tokens, out_grad):
    given = [experts, slots, logits, tokens, out_grad]

    def kernel(group_ref, *refs):
        count = len(given)
        ins, outs, flat_out = refs[:count], refs[count : count + SIDE], refs[count + SIDE]
        experts, slots, logits, tok, grad, sem = refs[count + SIDE + 1 :]
        loads = [
            pltpu.make_async_copy(a, b, sem.at[k])
            for k, (a, b) in enumerate(zip(ins, (experts, slots, logits, tok, grad)))
        ]
        for copy in loads:
            copy.start()
        for copy in loads:
            copy.wait()
        flat = lax.rem(experts[...] + (SIDE - group_ref[0]), SIDE) * CAP + slots[...]
        flat_out[...] = flat
        for j in range(SIDE):
            first, second, weight = choices(flat, logits[...], j)
            pick = jnp.where(first | second, 1.0, 0.0).astype(BF)
            weight = jnp.sum(weight, axis=1, keepdims=True)
            outs[j][:, :WIDE] = dot(pick, tok[...], ((1,), (1,))).astype(BF)
            outs[j][:, WIDE:] = (weight * dot(pick, grad[...], ((1,), (1,)))).astype(BF)

    whole = pl.BlockSpec(memory_space=pltpu.VMEM)
    return pl.pallas_call(
        kernel,
        in_specs=[pl.BlockSpec(memory_space=pltpu.SMEM)]
        + [pl.BlockSpec(memory_space=pl.ANY)] * len(given),
        out_specs=[whole] * (SIDE + 1),
        out_shape=[shape_of(CAP, 2 * WIDE)] * SIDE + [shape_of(*slots.shape, dtype=jnp.int32)],
        scratch_shapes=[pltpu.VMEM(a.shape, a.dtype) for a in given]
        + [pltpu.SemaphoreType.DMA((len(given),))],
        compiler_params=pltpu.CompilerParams(vmem_limit_bytes=62 * 1024 * 1024),
        cost_estimate=pl.CostEstimate(
            flops=4 * ROWS * 256 * WIDE, bytes_accessed=4 * ROWS * WIDE, transcendentals=0
        ),
        name="pack_rows",
    )(group, *given)


def assemble(order, parts):
    def kernel(_, *refs):
        cols = jnp.concatenate([r[...] for r in refs[:SIDE]], axis=0).T
        refs[SIDE][...] = cols[:WIDE]
        refs[SIDE + 1][...] = cols[WIDE:]

    return run(kernel, order, parts, [shape_of(WIDE, ROWS)] * 2, name="assemble_columns")


def arrange(order, gate, up, down, after):
    per = 4

    def kernel(order_ref, gate_in, up_in, down_in, gate_out, up_out, own_out, send_out):
        odd = lax.rem(order_ref[0], 2) == 1
        turned = down_in[...].T.reshape(per, 2, WIDE, HID)
        own_out[...] = jnp.where(odd, turned[:, 1], turned[:, 0])
        send_out[...] = jnp.where(odd, turned[:, 0], turned[:, 1])
        gate_out[...] = gate_in[...]
        up_out[...] = up_in[...]

    other = ((per, None, WIDE, HID), lambda i, order: (i, 1 - lax.rem(order[0], 2), 0, 0))
    out = (shape_of(BLOCKS // 2, WIDE, HID), (per, WIDE, HID), lambda i, order: (i, 0, 0))
    return run(
        kernel,
        order,
        [
            (gate.reshape(BLOCKS // 2, 2, WIDE, HID), *other),
            (up.reshape(BLOCKS // 2, 2, WIDE, HID), *other),
            (down, (HID, per * 2 * WIDE), lambda i, order: (0, i)),
        ],
        [out] * 4,
        steps=BLOCKS // 2 // per,
        after=after,
        name="arrange_weights",
    )


def contract(order, weights, chunks, totals, finish=None, after=()):
    steps = 2 * len(chunks)
    pieces, users = [], [[] for _ in range(steps)]
    for k, (_, own, other) in enumerate(chunks):
        for side in (own, other):
            if len(side) == 1:
                at = lambda i, order, k=k: (jnp.clip(i - 2 * k, 0, 1), 0, 0)
                pieces.append((side[0], (2, WIDE, ROWS), at))
                users[2 * k].append(len(pieces) - 1)
                users[2 * k + 1].append(len(pieces) - 1)
            else:
                for half, array in enumerate(side):
                    pieces.append(array)
                    users[2 * k + half].append(len(pieces) - 1)

    def place(i):
        at = chunks[0][0]
        for k in range(1, len(chunks)):
            at = jnp.where(i >= 2 * k, chunks[k][0], at)
        return at * SIDE + lax.rem(i, 2) * 2

    mats = []
    for own, other, divisor in weights:
        for base, array in ((0, own), (16, other)):
            for b in range(2):
                at = lambda i, order, base=base, b=b, divisor=divisor: (
                    order[base + place(i) + b] // divisor,
                    0,
                    0,
                )
                mats.append((array, (None, WIDE, HID), at))
    more = list(finish[1]) if finish else []
    results = list(finish[2]) if finish else [shape_of(HID, ROWS, dtype=F32)] * len(weights)
    cuts = np.cumsum([len(pieces), len(mats), len(totals), len(more), len(results)])

    def kernel(_, *refs):
        p, m, before, given, outs, held = (
            refs[a:b] for a, b in zip([0, *cuts], [*cuts, len(refs)])
        )
        held = held if finish else outs
        for s in range(steps):

            @pl.when(pl.program_id(0) == s)
            def _():
                piece = jnp.concatenate(
                    [p[u][...].reshape(2 * WIDE, ROWS) for u in users[s]], axis=0
                )
                for w in range(len(weights)):
                    mat = jnp.concatenate([r[...] for r in m[4 * w : 4 * w + 4]], axis=0)
                    total = dot(mat, piece, ((0,), (0,)))
                    if s > 0:
                        total += held[w][...]
                    elif totals:
                        total += before[w][...]
                    held[w][...] = total
                if finish and s == steps - 1:
                    finish[0](held, given, outs)

    return run(
        kernel,
        order,
        [*pieces, *mats, *totals, *more],
        results,
        steps=steps,
        after=after,
        scratch=[pltpu.VMEM((HID, ROWS), F32)] * len(weights) if finish else [],
        flops=len(weights) * len(chunks) * 16 * WIDE * HID * ROWS,
        name="contract_features",
    )


def activate(totals, given, outs):
    g, u = totals[0][...], totals[1][...]
    outs[0][...] = g
    outs[1][...] = u
    outs[2][...] = (g * jax.nn.sigmoid(g) * u).astype(BF)


def differentiate(totals, given, outs):
    hidden, gate, up = given
    g, hg = gate[...], totals[0][...]
    s = jax.nn.sigmoid(g)
    outs[0][0:HID] = (hg * up[...] * s * (1.0 + g * (1.0 - s))).astype(BF)
    outs[0][HID : 2 * HID] = (hg * g * s).astype(BF)
    product = hidden[...].astype(F32) * hg
    outs[0][2 * HID :] = jnp.sum(product.reshape(HID // EXTRA, EXTRA, ROWS), axis=0).astype(BF)


def expand(order, weights, acts, places, outs, store, more=(), after=(), *, name):
    pairs = len(weights)
    ins = list(acts)
    for place in places:
        for own, divisor, other in weights:
            for array, by in ((own, divisor), (other, 2)):
                for b in range(SIDE):
                    at = lambda i, order, n=SIDE * place + b, by=by: (order[n] // by, 0, 0)
                    ins.append((array, (None, WIDE, HID), at))
    per = pairs * 2 * SIDE
    first_more = len(ins)
    ins += list(more)

    def kernel(_, own, other, *refs):
        mats = refs[: first_more - 2]
        given = refs[first_more - 2 : first_more - 2 + len(more)]
        results = refs[first_more - 2 + len(more) :]
        act = jnp.concatenate(
            [a[w * HID : (w + 1) * HID] for w in range(pairs) for a in (own, other)], axis=0
        )
        tail = None
        if acts[0].shape[0] > pairs * HID:
            tail = own[pairs * HID :].astype(F32) + other[pairs * HID :].astype(F32)
        for k in range(len(places)):
            for b in range(SIDE):
                block = [mats[k * per + n * SIDE + b][...] for n in range(pairs * 2)]
                value = dot(jnp.concatenate(block, axis=1), act)
                store(k, b, value, tail, given, results)

    return run(
        kernel,
        order,
        ins,
        outs,
        after=after,
        flops=len(places) * pairs * 16 * WIDE * HID * ROWS,
        name=name,
    )


def combine(order, near_out, back, first, second):
    def kernel(_, near, own, *refs):
        for b in range(SIDE):
            got = refs[2 * (b // 2) : 2 * (b // 2) + 2]
            total = own[b].astype(F32) + sum(r[b % 2].astype(F32) for r in got)
            refs[SIDE + b][:WIDE] = near[b]
            refs[SIDE + b][WIDE:] = total.astype(BF)

    outs = [shape_of(2 * WIDE + EXTRA, ROWS)] * SIDE
    ins = [near_out, back, *first, *second]
    return run(kernel, order, ins, outs, name="combine_blocks")


def add(order, pairs, after):
    def kernel(_, *refs):
        for k in range(len(pairs)):
            total = refs[2 * k][...].astype(F32) + refs[2 * k + 1][...].astype(F32)
            refs[2 * len(pairs) + k][...] = total.astype(BF)

    outs = [shape_of(*p[0].shape) for p in pairs]
    ins = [a for p in pairs for a in p]
    return run(kernel, order, ins, outs, after=after, name="add_blocks")


def gather_sum(order, parts, after):
    both = 2 * WIDE

    def kernel(_, *refs):
        total = sum(r[...].astype(F32) for r in refs[:SIDE])
        rows = total[:both].astype(BF).T
        product = jnp.sum(total[both:], axis=0, keepdims=True)
        high = product.astype(BF)
        low = (product - high.astype(F32)).astype(BF)
        for j in range(SIDE):
            out, cut = refs[SIDE + j], slice(j * CAP, (j + 1) * CAP)
            out[:CAP] = rows[cut]
            line = lax.broadcasted_iota(jnp.int32, (EXTRA, CAP), 0)
            lines = jnp.where(line == 0, high[:, cut].astype(F32), 0.0) + jnp.where(
                line == 1, low[:, cut].astype(F32), 0.0
            )
            out[CAP:, :CAP] = lines.astype(BF)
            out[CAP:, CAP:] = jnp.zeros((EXTRA, both - CAP), BF)

    outs = [shape_of(CAP + EXTRA, both)] * SIDE
    return run(kernel, order, parts, outs, after=after, name="sum_rows")


def collect(order, flat, logits, parts):
    tokens = flat.shape[1]

    def kernel(_, flat, logits, *refs):
        got, (mixed, back, grads) = refs[:SIDE], refs[SIDE:]
        out, tok, product = 0.0, 0.0, [0.0, 0.0]
        for j in range(SIDE):
            first, second, weight = choices(flat[...], logits[...], j)
            high = weight.astype(BF)
            low = (weight - high.astype(F32)).astype(BF)
            picks = [jnp.where(pick, 1.0, 0.0).astype(BF) for pick in (first, second)]
            cols = got[j][:CAP].T
            out += dot(cols[:WIDE], high) + dot(cols[:WIDE], low)
            tok += dot(cols[WIDE:], picks[0]) + dot(cols[WIDE:], picks[1])
            for k in range(2):
                product[k] += dot(got[j][CAP:, :CAP], picks[k])
        mixed[...] = out.astype(BF)
        back[...] = tok.astype(BF)
        gap = logits[0:1, :] - logits[1:2, :]
        one, two = (jnp.sum(p, axis=0, keepdims=True) for p in product)
        cross = jax.nn.sigmoid(-gap) * one - jax.nn.sigmoid(gap) * two
        grads[...] = jnp.concatenate([cross, -cross], axis=0)

    return run(
        kernel,
        order,
        [flat, logits, *parts],
        [shape_of(WIDE, tokens), shape_of(WIDE, tokens), shape_of(2, tokens, dtype=F32)],
        flops=8 * tokens * ROWS * WIDE,
        name="collect_rows",
    )


PIECES = ((0, 4), (4, 4), (12, 4), (8, 4))
STARTS = [(base + first, n) for base in (0, 16) for first, n in PIECES]


def gradient_call(kernel, order, rows, pieces, outs, scratch, flops, name):
    moved = 2 * BLOCKS * WIDE * (ROWS + HID * len(outs))
    return pl.pallas_call(
        kernel,
        in_specs=[pl.BlockSpec(memory_space=pltpu.SMEM)]
        + [pl.BlockSpec(memory_space=pltpu.VMEM)] * (1 + len(pieces)),
        out_specs=[pl.BlockSpec(memory_space=pltpu.HBM)] * len(outs)
        + [pl.BlockSpec(memory_space=pltpu.VMEM)],
        out_shape=[*outs, shape_of(8, 128, dtype=F32)],
        scratch_shapes=scratch,
        compiler_params=pltpu.CompilerParams(vmem_limit_bytes=VMEM_LIMIT),
        cost_estimate=pl.CostEstimate(flops=flops, bytes_accessed=moved, transcendentals=0),
        name=name,
    )(order, rows, *pieces)


def weight_grads(order, pieces, rows):
    def kernel(order_ref, rows_ref, *refs):
        count = len(pieces)
        ins, outs, mark = refs[:count], refs[count : count + 2], refs[count + 2]
        done, sem = refs[count + 3 :]
        mark[...] = jnp.zeros(mark.shape, F32)
        stores = []
        act = rows_ref[: 2 * HID]
        for k, (first, n) in enumerate(STARTS):
            piece = ins[k][...].reshape(n * WIDE, ROWS)
            value = dot(piece, act, ((1,), (1,))).astype(BF).reshape(n, WIDE, 2 * HID)
            for w in range(2):
                done[w, first : first + n] = value[:, :, w * HID : (w + 1) * HID]
                for b in range(first, first + n):
                    stores.append(
                        pltpu.make_async_copy(
                            done.at[w, b], outs[w].at[order_ref[b]], sem.at[w, b]
                        )
                    )
                    stores[-1].start()
        for copy in stores:
            copy.wait()

    return gradient_call(
        kernel,
        order,
        rows,
        pieces,
        [shape_of(BLOCKS, WIDE, HID)] * 2,
        [pltpu.VMEM((2, BLOCKS, WIDE, HID), BF), pltpu.SemaphoreType.DMA((2, BLOCKS))],
        4 * BLOCKS * WIDE * HID * ROWS,
        "weight_gradients",
    )


def down_grads(order, pieces, hidden):
    def kernel(order_ref, hidden_ref, *refs):
        count = len(pieces)
        ins, out, mark = refs[:count], refs[count], refs[count + 1]
        placed, done, sem = refs[count + 2 :]
        mark[...] = jnp.zeros(mark.shape, F32)
        act = hidden_ref[...]
        for k, (first, n) in enumerate(STARTS):
            piece = ins[k][...].reshape(n * WIDE, ROWS)
            value = dot(piece, act, ((1,), (1,))).astype(BF).reshape(n, WIDE, HID)
            for b in range(n):
                placed[order_ref[first + b]] = value[b]
        stores = []
        for s in range(BLOCKS // 2):
            done[s] = placed[2 * s : 2 * s + 2].reshape(2 * WIDE, HID).T
            stores.append(
                pltpu.make_async_copy(
                    done.at[s], out.at[:, pl.ds(s * 2 * WIDE, 2 * WIDE)], sem.at[s]
                )
            )
            stores[-1].start()
        for copy in stores:
            copy.wait()

    return gradient_call(
        kernel,
        order,
        hidden,
        pieces,
        [shape_of(HID, BLOCKS * WIDE)],
        [
            pltpu.VMEM((BLOCKS, WIDE, HID), BF),
            pltpu.VMEM((BLOCKS // 2, HID, 2 * WIDE), BF),
            pltpu.SemaphoreType.DMA((BLOCKS // 2,)),
        ],
        2 * BLOCKS * WIDE * HID * ROWS,
        "down_gradients",
    )


def hold(arrays, after):
    def kernel(*refs):
        pass

    return pl.pallas_call(
        kernel,
        in_specs=[pl.BlockSpec(memory_space=pl.ANY)] * (len(arrays) + len(after)),
        out_specs=[pl.BlockSpec(memory_space=pl.ANY)] * len(arrays),
        out_shape=[jax.ShapeDtypeStruct(a.shape, a.dtype) for a in arrays],
        input_output_aliases={k: k for k in range(len(arrays))},
        compiler_params=pltpu.CompilerParams(vmem_limit_bytes=VMEM_LIMIT),
        cost_estimate=pl.CostEstimate(flops=0, bytes_accessed=0, transcendentals=0),
        name="hold",
    )(*arrays, *after)


def stack(order, blocks, after):
    def kernel(_, *refs):
        for j in range(SIDE):
            refs[SIDE][j] = refs[j][...]

    outs = [shape_of(SIDE, WIDE, ROWS)]
    return run(kernel, order, blocks, outs, after=after, name="stack_blocks")[0]


def join(order, far, after):
    def kernel(_, first, second, out):
        out[0:2] = first[...]
        out[2:4] = second[...]

    outs = [shape_of(SIDE, WIDE, ROWS)]
    return run(kernel, order, far, outs, after=after, name="join_blocks")[0]


def halves(order, arrived, after=()):
    def kernel(_, from_before, from_after, *outs):
        outs[0][...] = from_before[...]
        outs[1][...] = from_after[...]

    half = (2, WIDE, ROWS)
    return run(
        kernel,
        order,
        [(arrived[0], half, fixed(0, 0, 0)), (arrived[1], half, fixed(1, 0, 0))],
        [shape_of(*half)] * 2,
        after=after,
        name="half_blocks",
    )


def shards(
    tokens, expert_ids, slot_ids, route_logits, gate_weight, up_weight, down_weight, out_grad
):
    group, z, x, core = (lax.axis_index(a) for a in ("ep", "z", "x", "c"))
    logits = route_logits.T

    near, far = jnp.arange(16, dtype=jnp.int32) % SIDE, jnp.arange(16, dtype=jnp.int32) // SIDE

    def arrival(c):
        by_z = jnp.where(c == 0, near, far)
        by_x = jnp.where(c == 0, far, near)
        return (
            jnp.remainder(z - by_z, SIDE) * SIDE + jnp.remainder(x - by_x, SIDE)
        ) * 2 + c

    order = jnp.concatenate([arrival(core), arrival(1 - core)]).astype(jnp.int32)
    gate = gate_weight.reshape(BLOCKS, WIDE, HID)
    up = up_weight.reshape(BLOCKS, WIDE, HID)
    down = down_weight.reshape(HID, BLOCKS * WIDE)

    *packed, flat = pack(
        group.reshape(1), expert_ids.T, slot_ids.T, logits, tokens.T, out_grad.T
    )
    part_2, part_1, part_3 = (lax.ppermute(packed[j], "ep", ring(j)) for j in (2, 1, 3))
    parts = [packed[0], part_1, part_2, part_3]
    own_in, own_grad = assemble(order, parts)

    in_weights = [(gate, gate, 1), (up, up, 1)]
    first = [send(own_in, 1, k) for k in (1, 2, 3)]
    near_in = stack(order, [own_in, *first], [])
    gate_send, up_send, down_own, down_send = arrange(order, gate, up, down, [near_in])
    gate_x, up_x, down_x = swap(gate_send), swap(up_send), swap(down_send)
    first = [send(own_grad, 1, k) for k in (1, 2, 3)]
    near_grad = stack(order, [own_grad, *first], [near_in])
    near_in_x, near_grad_x = swap(near_in), swap(near_grad)
    in_1, in_3 = send(near_in, 2, 1), send(near_in, 2, 3)
    totals = contract(
        order,
        in_weights,
        [(0, [near_in], [near_in_x])],
        [],
        after=[gate_send, down_send, near_grad_x],
    )
    in_1, in_3 = hold([in_1, in_3], totals)
    in_a, in_b = halves(order, [in_1, in_3])
    in_2 = [send(in_a, 2, 1), send(in_b, 2, 3)]
    in_1x, in_3x = swap(in_1), swap(in_3)
    totals = contract(
        order, in_weights, [(1, [in_1], [in_1x]), (3, [in_3], [in_3x])], totals, after=[in_a, gate_x, up_x, down_x]
    )
    (near_grad,) = hold([near_grad], totals)
    grad_1, grad_3 = send(near_grad, 2, 1), send(near_grad, 2, 3)
    in_2 = join(order, in_2, totals)
    in_2x = swap(in_2)
    wide = shape_of(HID, ROWS, dtype=F32)
    gate_act, up_act, hidden = contract(
        order,
        in_weights,
        [(2, [in_2], [in_2x])],
        totals,
        (activate, [], [wide, wide, shape_of(HID, ROWS)]),
    )

    acts = (hidden, swap(hidden))
    out_weights = [(down_own, 2, down_x)]
    block4, block2 = shape_of(SIDE, WIDE, ROWS), shape_of(2, WIDE, ROWS)

    def split(k, b, value, tail, given, outs):
        outs[b // 2][b % 2] = value.astype(BF)

    def add_relayed(k, b, value, tail, given, outs):
        if b // 2 == k:
            value += given[k][b % 2].astype(F32)
        outs[k][b] = value.astype(BF)

    def add_last(k, b, value, tail, given, outs):
        outs[0][b] = (value + given[0][b].astype(F32) + given[1][b].astype(F32)).astype(BF)

    out_a, out_b = expand(
        order, out_weights, acts, [2], [block2] * 2, split, name="expert_out"
    )
    relayed = [send(out_a, 2, 3), send(out_b, 2, 1)]

    grad_1, grad_3 = hold([grad_1, grad_3], relayed)
    grad_a, grad_b = halves(order, [grad_1, grad_3])
    grad_2 = [send(grad_a, 2, 1), send(grad_b, 2, 3)]
    grad_1x, grad_3x = swap(grad_1), swap(grad_3)
    grad_weights = [(down_own, down_send, 2)]
    totals_grad = contract(
        order,
        grad_weights,
        [
            (0, [near_grad], [near_grad_x]),
            (1, [grad_1], [grad_1x]),
            (3, [grad_3], [grad_3x]),
        ],
        [],
        after=[grad_a],
    )

    out_1, out_3 = expand(
        order,
        out_weights,
        acts,
        [1, 3],
        [block4] * 2,
        add_relayed,
        relayed,
        name="expert_out",
    )
    arrived_out = [send(out_1, 2, 3), send(out_3, 2, 1)]
    grad_2 = join(order, grad_2, totals_grad)
    grad_2x = swap(grad_2)
    (rows,) = contract(
        order,
        grad_weights,
        [(2, [grad_2], [grad_2x])],
        totals_grad,
        (differentiate, [hidden, gate_act, up_act], [shape_of(2 * HID + EXTRA, ROWS)]),
        after=[out_1],
    )
    out_acts = acts
    acts = (rows, swap(rows))
    back_weights = [(gate, 1, gate_x), (up, 1, up_x)]
    tall = WIDE + EXTRA

    def plain(k, b, value, tail, given, outs):
        out = outs[2 * k + b // 2]
        out[b % 2, :WIDE] = value.astype(BF)
        out[b % 2, WIDE:] = tail.astype(BF)

    def own_four(k, b, value, tail, given, outs):
        outs[0][b, :WIDE] = value.astype(BF)
        outs[0][b, WIDE:] = tail.astype(BF)

    half = shape_of(2, tall, ROWS)
    back_2 = expand(order, back_weights, acts, [2], [half] * 2, plain, name="expert_back")
    relayed = [send(back_2[0], 2, 3), send(back_2[1], 2, 1)]
    low_1, high_1, low_3, high_3 = expand(
        order,
        back_weights,
        acts,
        [1, 3],
        [half] * 4,
        plain,
        [],
        [back_2[0]],
        name="expert_back",
    )
    early = [send(low_3, 2, 1), send(high_1, 2, 3)]
    (back_0,) = expand(
        order,
        back_weights,
        acts,
        [0],
        [shape_of(SIDE, tall, ROWS)],
        own_four,
        [],
        [low_1],
        name="expert_back",
    )
    (near_out,) = expand(
        order,
        out_weights,
        out_acts,
        [0],
        [block4],
        add_last,
        arrived_out,
        [back_0],
        name="expert_out",
    )
    low_1, high_3 = add(order, [(low_1, relayed[0]), (high_3, relayed[1])], [near_out])
    late = [send(low_1, 2, 3), send(high_3, 2, 1)]
    down_grad, done = down_grads(
        order,
        [near_grad, grad_1, grad_3, grad_2, near_grad_x, grad_1x, grad_3x, grad_2x],
        hold([hidden], [low_1, *early])[0],
    )
    late = hold(late, [done])
    sums = combine(order, near_out, back_0, [early[0], late[0]], [early[1], late[1]])

    parts = [sums[0]] + [send(sums[j], 1, SIDE - j) for j in (1, 2, 3)]
    gate_grad, up_grad, done = weight_grads(
        order,
        [near_in, in_1, in_3, in_2, near_in_x, in_1x, in_3x, in_2x],
        hold([rows], [sums[0]])[0],
    )
    sums = gather_sum(order, parts, [done])
    back = [sums[0]] + [lax.ppermute(sums[j], "ep", ring(SIDE - j)) for j in (1, 2, 3)]
    mixed, token_grad, logit_grad = collect(order, flat, logits, back)
    return (
        mixed.T,
        token_grad.T,
        logit_grad.T,
        gate_grad.reshape(gate_weight.shape),
        up_grad.reshape(up_weight.shape),
        down_grad.reshape(down_weight.shape),
    )


def solution(mesh):
    tp = ("z", "x", "c")
    fine = Mesh(mesh.devices.reshape(SIDE, SIDE, SIDE, 2), ("ep", *tp))
    return jax.shard_map(
        shards,
        mesh=fine,
        in_specs=(
            P("ep", tp),
            P("ep", None),
            P("ep", None),
            P("ep", None),
            P("ep", None, tp),
            P("ep", None, tp),
            P("ep", tp, None),
            P("ep", tp),
        ),
        out_specs=(
            P("ep", tp),
            P("ep", tp),
            P("ep", None),
            P("ep", None, tp),
            P("ep", None, tp),
            P("ep", tp, None),
        ),
        check_vma=False,
    )
```
